512 devices in a mesh: band: 32 (over x, y), lev: 16 (over z, core).
Axes of the slice: x: 4, y: 8, z: 8, core: 2. Of those that a mesh axis runs over, the one named last changes fastest.
Arguments:
- increment: bfloat16 [2, 128, 1024, 128], P(None, 'lev', 'band'), may hold values from -6 to 6
- diffusivity: bfloat16 [2, 128, 1024, 128], P(None, 'lev', 'band'), may hold values from 0.049804688 to 0.15917969
- sigma: bfloat16 [2, 128, 1024, 128], P(None, 'lev', 'band'), may hold values from 0.5 to 2
- jacobian: bfloat16 [4, 256, 2, 128], P(None, None, None, 'lev'), may hold values from -0.375 to 0.375
- rinv: float32 [256], replicated, may hold values from 0.25 to 4
- innovation: bfloat16 [32, 256, 32, 128], P('band'), may hold values from -6 to 6
- obs_column: int32 [32, 32, 128], P('band'), may hold values from 0 to 4095
- obs_table: int32 [32, 32, 128], P('band'), may hold values from 0 to 3
- obs_count: int32 [32, 32], P('band'), may hold values from 0 to 128, as said below
Outputs:
- gradient: float32 [2, 128, 1024, 128], P(None, 'lev', 'band')
The draws below stay inside these ranges and needn't reach their ends.
Inputs may be any that keep to these rules, and one draw needn't show every extreme that they name: The profiles that owner o takes from band s fill its first obs_count[o, s] slots of that band; the most, 128, is reached by every owner from some band and by one owner from every band.
All inputs are finite; a program needn't handle non-finite values.
Results may differ from the reference program's by a relative error of at most 0.006.
Values may be sent and summed in bfloat16 or wider, within the bound.
A program may use at most 64 MiB of HBM per device.

```python
import math
import jax
import jax.numpy as jnp
from jax import lax

FIELDS = 2
CH = 256
NTAB = 4
STEPS = 3
LEV_DEV = 8
LON_DEV = 32
LAT = 128
BANDS = 32
CAP = 128
LEVELS = 128
LON = 1024
N_LEV = 16


def draw_obs_count(key, part):
    key_base = jax.random.fold_in(key, 11)
    key_hot = jax.random.fold_in(key, 12)
    key_full = jax.random.fold_in(key, 13)
    base = jax.random.randint(key_base, (BANDS, BANDS), CAP // 8, CAP // 2 + 1)
    hot_start = jax.random.randint(key_hot, (), 0, BANDS)
    full_owner = jax.random.randint(key_full, (), 0, BANDS)
    source = jnp.arange(BANDS, dtype=jnp.int32)[None, :]
    owner = jnp.arange(BANDS, dtype=jnp.int32)[:, None]
    hot = (source - hot_start) % BANDS < max(BANDS // 8, 1)
    full = owner == full_owner
    return jnp.where(hot | full, CAP, base).astype(jnp.int32)


def touch_ends(array, own_key, low, top_value):
    longest = array.shape.index(max(array.shape))
    spots = []
    for shift in (0, 1):
        where = [jax.random.randint(jax.random.fold_in(own_key, axis), (), 0, length) for axis, length in enumerate(array.shape)]
        where[longest] = (where[longest] + shift) % array.shape[longest]
        spots.append(tuple(where))
    return array.at[spots[0]].set(low).at[spots[1]].set(top_value)


def shard_levels(stream_key, dims, cuts, smallest, high):
    def one(axis_at, parts):
        draws = jax.random.uniform(jax.random.fold_in(jax.random.fold_in(stream_key, 6), axis_at), (parts,), jnp.float32, smallest / len(cuts), high / len(cuts))
        return jnp.repeat(jnp.exp(draws), dims[axis_at] // parts).reshape((-1,) + (1,) * (len(dims) - axis_at - 1))

    gain = one(*cuts[0])
    for cut in cuts[1:]:
        gain = gain * one(*cut)
    return gain


def normal_values(rng, dims, spread, reach, cuts=(), held_as=jnp.bfloat16):
    level = shard_levels(rng, dims, cuts, -0.22, 0.18) if cuts else 1.0
    entries = jax.random.normal(rng, dims, jnp.float32) * spread * level
    return jnp.minimum(jnp.maximum(entries, -reach), reach).astype(held_as)


def setup_inputs(seed: int = 0) -> dict:
    keys = jax.random.split(jax.random.key(seed), 10)
    increment = normal_values(keys[0], (FIELDS, LEVELS, LON, LAT), 1.0, 6.0, ((1, 16), (2, 32)))
    diffusivity = jnp.clip(jnp.exp(math.log(0.15917969) - 1.1619246 * jax.random.uniform(keys[1], (FIELDS, LEVELS, LON, LAT), jnp.float32) ** shard_levels(keys[1], (FIELDS, LEVELS, LON, LAT), ((1, 16), (2, 32)), -0.2, 0.2)), 0.049804688, 0.15917969).astype(jnp.bfloat16)
    sigma = jnp.clip(jnp.exp(math.log(2.0) - 1.3862944 * jax.random.uniform(keys[2], (FIELDS, LEVELS, LON, LAT), jnp.float32) ** shard_levels(keys[2], (FIELDS, LEVELS, LON, LAT), ((1, 16), (2, 32)), -0.2, 0.2)), 0.5, 2.0).astype(jnp.bfloat16)
    jacobian = normal_values(keys[3], (NTAB, CH, FIELDS, LEVELS), (FIELDS * LEVELS) ** -0.5, 0.375, ((3, 16),))
    rinv = jnp.clip(jnp.exp(jax.random.uniform(keys[4], (CH,), jnp.float32, math.log(0.25), math.log(4.0))), 0.25, 4.0)
    innovation = normal_values(keys[5], (BANDS, CH, BANDS, CAP), 1.0, 6.0, ((0, 32),))
    obs_column = touch_ends(jax.random.randint(keys[6], (BANDS, BANDS, CAP), 0, LON_DEV * LAT), jax.random.fold_in(keys[6], 1), 0, (LON_DEV * LAT) - 1).astype(jnp.int32)
    obs_table = touch_ends(jax.random.randint(keys[7], (BANDS, BANDS, CAP), 0, NTAB), jax.random.fold_in(keys[7], 1), 0, NTAB - 1).astype(jnp.int32)
    obs_count = draw_obs_count(jax.random.fold_in(keys[9], 71), 0)
    return dict(increment=increment, diffusivity=diffusivity, sigma=sigma, jacobian=jacobian, rinv=rinv, innovation=innovation, obs_column=obs_column, obs_table=obs_table, obs_count=obs_count)


def lap(a):
    padded = jnp.pad(a, ((0, 0), (1, 1), (0, 0), (1, 1)))
    total = padded[:, 2:, :, 1:-1] + padded[:, :-2, :, 1:-1]
    total = total + jnp.roll(a, 1, axis=2) + jnp.roll(a, -1, axis=2)
    total = total + padded[:, 1:-1, :, 2:] + padded[:, 1:-1, :, :-2]
    return total - 6.0 * a


def reference(increment, diffusivity, sigma, jacobian, rinv, innovation, obs_column, obs_table, obs_count):
    coeff = diffusivity.astype(jnp.float32)
    scale = sigma.astype(jnp.float32)
    field = increment.astype(jnp.float32)
    for step in range(STEPS):
        field = field + coeff * lap(field)
    state = (scale * field).astype(jnp.bfloat16)
    source = jnp.arange(BANDS, dtype=jnp.int32)[:, None, None]
    global_col = (source * LON_DEV + obs_column // LAT) * LAT + obs_column % LAT
    owner_cols = jnp.transpose(global_col, (1, 0, 2)).reshape(-1)
    tables = obs_table.reshape(-1)
    slot_ids = jnp.arange(CAP, dtype=jnp.int32)
    valid = (slot_ids[None, None, :] < obs_count[:, :, None]).reshape(-1)
    observed = jnp.transpose(innovation, (1, 0, 2, 3)).reshape(CH, -1).astype(jnp.float32)
    columns = state.reshape(FIELDS, LEVELS, LON * LAT)
    width = FIELDS * LEV_DEV

    def group_weights(group):
        return lax.dynamic_slice_in_dim(jacobian, group * LEV_DEV, LEV_DEV, 3).reshape(NTAB, CH, width)

    def forward_group(total, group):
        block = lax.dynamic_slice_in_dim(columns, group * LEV_DEV, LEV_DEV, 1).reshape(width, LON * LAT)
        profile = jnp.take(block, owner_cols, axis=1)
        weights = group_weights(group)
        partial_value = jnp.zeros((CH, owner_cols.shape[0]), jnp.float32)
        for table in range(NTAB):
            product = jnp.dot(weights[table], profile, preferred_element_type=jnp.float32)
            partial_value = partial_value + jnp.where(tables[None, :] == table, product, 0.0)
        rounded = lax.optimization_barrier(partial_value.astype(jnp.bfloat16))
        return total + rounded.astype(jnp.float32), None

    groups = jnp.arange(N_LEV, dtype=jnp.int32)
    evolved, unused = lax.scan(forward_group, jnp.zeros((CH, owner_cols.shape[0]), jnp.float32), groups)
    resid = jnp.where(valid[None, :], rinv[:, None] * (evolved - observed), 0.0).astype(jnp.bfloat16)

    def adjoint_group(group):
        weights = group_weights(group)
        back = jnp.zeros((width, owner_cols.shape[0]), jnp.float32)
        for table in range(NTAB):
            masked = jnp.where(tables[None, :] == table, resid, jnp.zeros_like(resid))
            back = back + jnp.dot(weights[table].T, masked, preferred_element_type=jnp.float32)
        rounded = lax.optimization_barrier(back.astype(jnp.bfloat16))
        return jnp.zeros((width, LON * LAT), jnp.float32).at[:, owner_cols].add(rounded.astype(jnp.float32))

    mapped = lax.map(adjoint_group, groups)
    adjoint = mapped.reshape(N_LEV, FIELDS, LEV_DEV, LON * LAT).transpose(1, 0, 2, 3).reshape(FIELDS, LEVELS, LON, LAT)
    field = scale * adjoint
    for step in range(STEPS):
        field = field + lap(coeff * field)
    return increment.astype(jnp.float32) + field
```

```python
import functools

import jax
import jax.numpy as jnp
from jax import lax
from jax.experimental import pallas as pl
from jax.experimental.pallas import tpu as pltpu
from jax.sharding import PartitionSpec as P

MESH = pl.DeviceIdType.MESH
F32 = jnp.float32
BF16 = jnp.bfloat16

NTAB = 4
STEPS = 3
HALO = 3
FIELDS = 2
LEV = 8
LON = 32
LAT = 128
CAP = 128
ROWS = LON + 8
EXT = LEV + 2 * HALO
WIDTH = FIELDS * LEV
PAIR = 2 * CAP


def dot(a, b, dims):
    return lax.dot_general(a, b, (dims, ((), ())), preferred_element_type=F32)


def kernel(
    nb,
    ng,
    inc_hbm,
    dif_hbm,
    sig_hbm,
    jac_hbm,
    rinv_ref,
    inn_hbm,
    col_hbm,
    tab_hbm,
    cnt_ref,
    out_ref,
    inc_e,
    dif_e,
    sig_v,
    col_v,
    tab_v,
    inn_v,
    inn_f,
    inn_s,
    pack,
    lon_r,
    pack_w,
    lon_w,
    w_e,
    dfx,
    ua,
    ub,
    uc,
    st,
    s_mat,
    hot,
    a_mat,
    adj,
    prof,
    arr,
    junk,
    tabs,
    tabs_t,
    rcol,
    back,
    home,
    load_sem,
    halo_send,
    halo_recv,
    w_send,
    w_recv,
    tab_sem,
    x_sem,
):
    b, g = lax.axis_index("band"), lax.axis_index("lev")
    per = nb // ng
    nz = ng // 2
    z, core = g // 2, g % 2
    left, right = lax.rem(b + nb - 1, nb), lax.rem(b + 1, nb)
    hub = b // per
    has_low, has_high = g > 0, g < ng - 1

    loads = [
        pltpu.make_async_copy(inc_hbm, inc_e.at[:, HALO : HALO + LEV], load_sem.at[0]),
        pltpu.make_async_copy(dif_hbm, dif_e.at[:, HALO : HALO + LEV], load_sem.at[1]),
        pltpu.make_async_copy(sig_hbm, sig_v, load_sem.at[2]),
        pltpu.make_async_copy(col_hbm.at[0], col_v, load_sem.at[3]),
        pltpu.make_async_copy(tab_hbm.at[0], tab_v, load_sem.at[4]),
        pltpu.make_async_copy(
            inn_hbm.at[0, :, pl.ds(pl.multiple_of((per * g) // 16 * 16, 16), 16)],
            inn_v,
            load_sem.at[5],
        ),
    ]
    for load in loads:
        load.start()

    barrier = pltpu.get_barrier_semaphore()

    def greet(band, lev):
        pl.semaphore_signal(barrier, inc=1, device_id=(band, lev), device_id_type=MESH)

    for side in (left, right):
        greet(side, g)
    for has, lev in ((has_low, g - 1), (has_high, g + 1)):

        @pl.when(has)
        def _():
            for side in (left, b, right):
                greet(side, lev)

    @pl.loop(0, nz)
    def _(other):
        @pl.when(other != z)
        def _():
            greet(b, 2 * other + core)

    @pl.loop(0, per * ng)
    def _(index):
        band, lev = per * g + index // ng, index % ng

        @pl.when(jnp.logical_or(band != b, lev != g))
        def _():
            greet(band, lev)

    zeros = jnp.zeros((FIELDS, HALO, LON, LAT), BF16)

    @pl.when(g == 0)
    def _():
        inc_e[:, 0:HALO] = zeros
        dif_e[:, 0:HALO] = zeros
        w_e[:, 0:HALO] = zeros
        lon_r[:, 0:HALO] = jnp.zeros((2, HALO, 16, LAT), BF16)
        lon_w[:, 0:HALO] = jnp.zeros((2, HALO, 16, LAT), BF16)

    @pl.when(g == ng - 1)
    def _():
        inc_e[:, EXT - HALO :] = zeros
        dif_e[:, EXT - HALO :] = zeros
        w_e[:, EXT - HALO :] = zeros
        lon_r[:, EXT - HALO :] = jnp.zeros((2, HALO, 16, LAT), BF16)
        lon_w[:, EXT - HALO :] = jnp.zeros((2, HALO, 16, LAT), BF16)

    for e in (0, EXT - 1):
        lon_r[:, e] = jnp.zeros((2, 16, LAT), BF16)
        lon_w[:, e] = jnp.zeros((2, 16, LAT), BF16)

    sub = lax.broadcasted_iota(jnp.int32, (8, LAT), 0)
    upper = sub < 4
    loads[0].wait()
    loads[1].wait()

    def pack_level(l):
        for side in (0, 1):
            tiles = []
            for f in range(FIELDS):
                x = inc_e[f, HALO + l].astype(F32)
                d = dif_e[f, HALO + l].astype(F32)
                if side == 0:
                    tile = jnp.where(upper, x[0:8], pltpu.roll(d[0:8], 4, 0))
                else:
                    tile = jnp.where(upper, pltpu.roll(d[LON - 8 :], 4, 0), x[LON - 8 :])
                tiles.append(tile)
            pack[side, l] = jnp.concatenate(tiles, axis=0).astype(BF16)

    pl.loop(0, LEV)(pack_level)

    senders = (
        2
        + 3 * has_low.astype(jnp.int32)
        + 3 * has_high.astype(jnp.int32)
        + (nz - 1)
        + nb
        - (g == hub).astype(jnp.int32)
    )
    pl.semaphore_wait(barrier, senders)

    def halo_copies(strips, lon_to, lev_pairs, send, recv):
        def copy(k, src, dst, band, lev):
            return pltpu.make_async_remote_copy(
                src_ref=src,
                dst_ref=dst,
                send_sem=send.at[k],
                recv_sem=recv.at[k],
                device_id=(band, lev),
                device_id_type=MESH,
            )

        level, up, down = [], [], []
        sides = (left, right)
        for k in (0, 1):
            level.append(copy(k, strips.at[k], lon_to.at[k, HALO : HALO + LEV], sides[k], g))
            up.append(copy(2 + k, strips.at[k, LEV - 2 :], lon_to.at[k, 1:HALO], sides[k], g + 1))
            down.append(
                copy(4 + k, strips.at[k, 0:2], lon_to.at[k, EXT - HALO : EXT - 1], sides[k], g - 1)
            )
        for i, (src, base, dst) in enumerate(lev_pairs):
            up.append(
                copy(6 + i, src.at[:, base + LEV - HALO : base + LEV], dst.at[:, 0:HALO], b, g + 1)
            )
            down.append(
                copy(8 + i, src.at[:, base : base + HALO], dst.at[:, EXT - HALO :], b, g - 1)
            )
        return level, up, down

    def halo_start(level, up, down):
        for has, copies in ((has_high, up), (has_low, down)):

            @pl.when(has)
            def _():
                for c in reversed(copies):
                    c.start()

        for c in level:
            c.start()

    def halo_arrive(level, up, down):
        for c in level:
            c.wait_recv()
        for has, copies in ((has_low, up), (has_high, down)):

            @pl.when(has)
            def _():
                for c in copies:
                    c.wait_recv()

    def halo_sent(level, up, down):
        for c in level:
            c.wait_send()
        for has, copies in ((has_high, up), (has_low, down)):

            @pl.when(has)
            def _():
                for c in copies:
                    c.wait_send()

    halo = halo_copies(
        pack, lon_r, ((inc_hbm, 0, inc_e), (dif_hbm, 0, dif_e)), halo_send, halo_recv
    )
    halo_start(*halo)

    own_tab = pltpu.make_async_copy(jac_hbm, tabs.at[core, z], tab_sem.at[1])
    own_tab.start()

    @pl.loop(0, nz)
    def _(other):
        @pl.when(other != z)
        def _():
            pltpu.make_async_remote_copy(
                src_ref=jac_hbm,
                dst_ref=tabs.at[core, z],
                send_sem=tab_sem.at[0],
                recv_sem=tab_sem.at[1],
                device_id=(b, 2 * other + core),
                device_id_type=MESH,
            ).start()

    loads[3].wait()

    def col_row(i):
        return jnp.concatenate([col_v[pl.ds(2 * i, 1)], col_v[pl.ds(2 * i + 1, 1)]], axis=1)

    def lon_low(cols):
        return lax.shift_right_logical(cols, 7) & 15

    def build_hot(i):
        cols = col_row(i)
        want = (lax.shift_right_logical(cols, 11) & 1) * LAT + (cols & (LAT - 1))
        iota = lax.broadcasted_iota(jnp.int32, (2 * LAT, PAIR), 0)
        hot[:, pl.ds(pl.multiple_of(i * PAIR, PAIR), PAIR)] = jnp.where(
            iota == want, 1.0, 0.0
        ).astype(BF16)

    pl.loop(0, nb // 2)(build_hot)

    halo_arrive(*halo)

    def widen(f, e):
        first = lon_r[0, e].astype(F32)
        last = lon_r[1, e].astype(F32)
        for k in range(FIELDS):

            @pl.when(f == k)
            def _():
                r = first[8 * k : 8 * k + 8]
                l = last[8 * k : 8 * k + 8]
                ua[k, e, LON:] = jnp.where(upper, r, l)
                dfx[k, e, LON:] = pltpu.roll(jnp.where(upper, l, r), 4, 0)

        ua[f, e, 0:LON] = inc_e[f, e].astype(F32)
        dfx[f, e, 0:LON] = dif_e[f, e].astype(F32)

    for f in range(FIELDS):
        pl.loop(0, EXT)(functools.partial(widen, f))

    lane = lax.broadcasted_iota(jnp.int32, (ROWS, LAT), 1)

    def lap(ref, f, e):
        c = ref[f, e]
        total = ref[f, e - 1] + ref[f, e + 1]
        total = total + (pltpu.roll(c, 1, 0) + pltpu.roll(c, ROWS - 1, 0))
        total = total + jnp.where(lane == 0, 0.0, pltpu.roll(c, 1, 1))
        total = total + jnp.where(lane == LAT - 1, 0.0, pltpu.roll(c, LAT - 1, 1))
        return total - 6.0 * c

    def forward(src, dst, step):
        def body(e):
            for f in range(FIELDS):
                dst[f, e] = src[f, e] + dfx[f, e] * lap(src, f, e)

        pl.loop(step, EXT - step)(body)

    forward(ua, ub, 1)
    forward(ub, ua, 2)
    loads[2].wait()

    def last_step(l):
        for f in range(FIELDS):
            e = l + HALO
            field = (ua[f, e] + dfx[f, e] * lap(ua, f, e))[0:LON]
            st[pl.ds(pl.multiple_of((f * LEV + l) * LON, LON), LON)] = (
                sig_v[f, l].astype(F32) * field
            )

    pl.loop(0, LEV)(last_step)

    for lon in range(LON):
        parts = [st[pl.ds(f * LEV * LON + lon, LEV, stride=LON)] for f in range(FIELDS)]
        s_mat[
            (lon % 16) * WIDTH : (lon % 16 + 1) * WIDTH, (lon // 16) * LAT : (lon // 16 + 1) * LAT
        ] = jnp.concatenate(parts, axis=0).astype(BF16)

    def gather(i):
        cols = col_row(i)
        low = lon_low(cols)
        chunk = hot[:, pl.ds(pl.multiple_of(i * PAIR, PAIR), PAIR)]
        rows = dot(s_mat[...], chunk, ((1,), (0,)))
        total = jnp.zeros((WIDTH, PAIR), F32)
        for k in range(16):
            total = jnp.where(low == k, rows[k * WIDTH : (k + 1) * WIDTH], total)
        total = total.astype(BF16)
        for half in range(2):
            owner = 2 * i + half
            prof[owner] = total[:, half * CAP : (half + 1) * CAP]
            here = jnp.logical_and(owner == b, g == hub)
            slot = arr.at[b % per, core, z]

            @pl.when(here)
            def _():
                pltpu.make_async_copy(prof.at[owner], slot, x_sem.at[1]).start()
                pltpu.make_async_copy(prof.at[owner], junk.at[0], x_sem.at[0]).start()

            @pl.when(jnp.logical_not(here))
            def _():
                pltpu.make_async_remote_copy(
                    src_ref=prof.at[owner],
                    dst_ref=slot,
                    send_sem=x_sem.at[0],
                    recv_sem=x_sem.at[1],
                    device_id=(owner, hub),
                    device_id_type=MESH,
                ).start()

    pl.loop(0, nb // 2)(gather)

    pltpu.make_async_copy(tabs.at[0], tabs.at[0], tab_sem.at[1]).wait()
    share = pltpu.make_async_remote_copy(
        src_ref=tabs.at[core],
        dst_ref=tabs.at[core],
        send_sem=tab_sem.at[2],
        recv_sem=tab_sem.at[3],
        device_id=(b, g + 1 - 2 * core),
        device_id_type=MESH,
    )
    share.start()

    loads[5].wait()
    loads[4].wait()

    def spread_inn(i):
        at = pl.ds(pl.multiple_of(i * 8, 8), 8)
        inn_f[pl.ds(pl.multiple_of(i * 128, 128), 128)] = (
            inn_v[at].astype(F32).reshape(128, CAP)
        )

    channels = inn_v.shape[0]
    pl.loop(0, channels // 8)(spread_inn)
    row = lax.rem(per * g, 16)
    for j in range(per):
        for i in range(channels // 8):
            inn_s[8 * i : 8 * i + 8, j * CAP : (j + 1) * CAP] = inn_f[
                pl.ds(i * 128 + row + j, 8, stride=16)
            ]
    for i in range(channels // 128):
        line = rinv_ref[:, i * 128 : (i + 1) * 128]
        rcol[i * 128 : (i + 1) * 128] = jnp.broadcast_to(line, (128, 128)).T

    pltpu.make_async_copy(tabs.at[0], tabs.at[0], tab_sem.at[3]).wait()

    def table(t):
        return tabs[:, :, t].reshape(ng * WIDTH, channels)

    for t in range(NTAB):
        tabs_t[t] = table(t).T

    pltpu.make_async_copy(arr, arr, x_sem.at[1]).wait()
    profiles = jnp.concatenate(
        [arr[j].reshape(ng * WIDTH, CAP) for j in range(per)], axis=1
    )
    kinds = jnp.concatenate([tab_v[pl.ds(per * g + j, 1)] for j in range(per)], axis=1)
    slot_id = lax.broadcasted_iota(jnp.int32, (1, CAP), 1)
    valid = jnp.concatenate(
        [(slot_id < cnt_ref[0, per * g + j]).astype(jnp.int32) for j in range(per)], axis=1
    )
    evolved = jnp.zeros((channels, per * CAP), F32)
    for t in range(NTAB):
        evolved = jnp.where(kinds == t, dot(tabs_t[t], profiles, ((1,), (0,))), evolved)
    scale = jnp.concatenate([rcol[...]] * per, axis=1)
    resid = jnp.where(valid > 0, scale * (evolved - inn_s[...]), 0.0)
    total = jnp.zeros((ng * WIDTH, per * CAP), F32)
    for t in range(NTAB):
        masked = jnp.where(kinds == t, resid, 0.0).astype(BF16)
        total = total + dot(table(t), masked, ((1,), (0,)))
    for j in range(per):
        back[j] = (
            total[:, j * CAP : (j + 1) * CAP].astype(BF16).reshape(2, nz, WIDTH, CAP)
        )

    @pl.loop(0, per * ng)
    def _(index):
        j, lev = index // ng, index % ng
        band = per * g + j
        here = jnp.logical_and(band == b, lev == g)
        src = back.at[j, lev % 2, lev // 2]

        @pl.when(here)
        def _():
            pltpu.make_async_copy(src, home.at[b], x_sem.at[3]).start()
            pltpu.make_async_copy(src, junk.at[1], x_sem.at[2]).start()

        @pl.when(jnp.logical_not(here))
        def _():
            pltpu.make_async_remote_copy(
                src_ref=src,
                dst_ref=home.at[b],
                send_sem=x_sem.at[2],
                recv_sem=x_sem.at[3],
                device_id=(band, lev),
                device_id_type=MESH,
            ).start()

    pltpu.make_async_copy(home, home, x_sem.at[3]).wait()

    def spread_home(i):
        low = lon_low(col_row(i))
        block = jnp.concatenate([home[2 * i], home[2 * i + 1]], axis=1).astype(F32)
        at = pl.ds(pl.multiple_of(i * PAIR, PAIR), PAIR)
        for k in range(16):
            a_mat[k * WIDTH : (k + 1) * WIDTH, at] = jnp.where(low == k, block, 0.0).astype(BF16)

    pl.loop(0, nb // 2)(spread_home)
    sums = dot(a_mat[...], hot[...], ((1,), (1,)))
    for k in range(2):
        adj[k * 256 : (k + 1) * 256] = sums[:, k * LAT : (k + 1) * LAT]

    for l in range(LEV):
        firsts, lasts = [], []
        for f in range(FIELDS):
            for i in range(LON // 8):
                cells = adj[pl.ds(i * 8 * WIDTH + f * LEV + l, 8, stride=WIDTH)]
                w = sig_v[f, l, 8 * i : 8 * i + 8].astype(F32) * cells
                ua[f, HALO + l, 8 * i : 8 * i + 8] = w
                if i == 0:
                    firsts.append(w)
                if i == LON // 8 - 1:
                    lasts.append(w)
        pack_w[0, l] = jnp.concatenate(firsts, axis=0).astype(BF16)
        pack_w[1, l] = jnp.concatenate(lasts, axis=0).astype(BF16)
        for f in range(FIELDS):
            w_e[f, HALO + l] = ua[f, HALO + l, 0:LON].astype(BF16)

    halo2 = halo_copies(pack_w, lon_w, ((w_e, HALO, w_e),), w_send, w_recv)
    halo_start(*halo2)
    halo_arrive(*halo2)

    def widen_w(e):
        first = lon_w[0, e].astype(F32)
        last = lon_w[1, e].astype(F32)
        for f in range(FIELDS):
            ua[f, e, LON:] = jnp.where(upper, first[8 * f : 8 * f + 8], last[8 * f : 8 * f + 8])

    pl.loop(0, EXT)(widen_w)
    for f in range(FIELDS):
        for e in (0, 1, 2, EXT - 3, EXT - 2, EXT - 1):
            ua[f, e, 0:LON] = w_e[f, e].astype(F32)

    def scale_all(e):
        for f in range(FIELDS):
            ub[f, e] = dfx[f, e] * ua[f, e]

    pl.loop(0, EXT)(scale_all)

    def backward(src, dst, step):
        def body(e):
            for f in range(FIELDS):
                w = ua[f, e] + lap(src, f, e)
                ua[f, e] = w
                dst[f, e] = dfx[f, e] * w

        pl.loop(step, EXT - step)(body)

    backward(ub, uc, 1)
    backward(uc, ub, 2)

    def finish(l):
        for f in range(FIELDS):
            e = l + HALO
            w = (ua[f, e] + lap(ub, f, e))[0:LON]
            out_ref[f, l] = inc_e[f, e].astype(F32) + w

    pl.loop(0, LEV)(finish)

    halo_sent(*halo)
    halo_sent(*halo2)
    if nz > 1:
        gone = tabs.at[0, 0 : nz - 1]
        pltpu.make_async_copy(gone, gone, tab_sem.at[0]).wait()
    share.wait_send()
    pltpu.make_async_copy(prof, prof, x_sem.at[0]).wait()
    pltpu.make_async_copy(back, back, x_sem.at[2]).wait()


def body(
    nb,
    ng,
    increment,
    diffusivity,
    sigma,
    jacobian,
    rinv,
    innovation,
    obs_column,
    obs_table,
    obs_count,
):
    channels = jacobian.shape[1]
    tables = jnp.transpose(jacobian, (0, 2, 3, 1)).reshape(NTAB, WIDTH, channels)
    per, nz = nb // ng, ng // 2
    hbm = pl.BlockSpec(memory_space=pl.ANY)
    vmem = pl.BlockSpec(memory_space=pltpu.VMEM)
    smem = pl.BlockSpec(memory_space=pltpu.SMEM)
    dma = pltpu.SemaphoreType.DMA
    extended = pltpu.VMEM((FIELDS, EXT, LON, LAT), BF16)
    wide = pltpu.VMEM((FIELDS, EXT, ROWS, LAT), F32)
    return pl.pallas_call(
        functools.partial(kernel, nb, ng),
        out_shape=jax.ShapeDtypeStruct((FIELDS, LEV, LON, LAT), F32),
        in_specs=[hbm, hbm, hbm, hbm, vmem, hbm, hbm, hbm, smem],
        out_specs=vmem,
        scratch_shapes=[
            extended,
            extended,
            pltpu.VMEM((FIELDS, LEV, LON, LAT), BF16),
            pltpu.VMEM((nb, CAP), jnp.int32),
            pltpu.VMEM((nb, CAP), jnp.int32),
            pltpu.VMEM((channels, 16, CAP), BF16),
            pltpu.VMEM((channels * 16, CAP), F32),
            pltpu.VMEM((channels, per * CAP), F32),
            pltpu.VMEM((2, LEV, 16, LAT), BF16),
            pltpu.VMEM((2, EXT, 16, LAT), BF16),
            pltpu.VMEM((2, LEV, 16, LAT), BF16),
            pltpu.VMEM((2, EXT, 16, LAT), BF16),
            extended,
            wide,
            wide,
            wide,
            wide,
            pltpu.VMEM((WIDTH * LON, LAT), F32),
            pltpu.VMEM((16 * WIDTH, 2 * LAT), BF16),
            pltpu.VMEM((2 * LAT, nb * CAP), BF16),
            pltpu.VMEM((16 * WIDTH, nb * CAP), BF16),
            pltpu.VMEM((WIDTH * LON, LAT), F32),
            pltpu.VMEM((nb, WIDTH, CAP), BF16),
            pltpu.VMEM((per, 2, nz, WIDTH, CAP), BF16),
            pltpu.VMEM((2, WIDTH, CAP), BF16),
            pltpu.VMEM((2, nz, NTAB, WIDTH, channels), BF16),
            pltpu.VMEM((NTAB, channels, ng * WIDTH), BF16),
            pltpu.VMEM((channels, CAP), F32),
            pltpu.VMEM((per, 2, nz, WIDTH, CAP), BF16),
            pltpu.VMEM((nb, WIDTH, CAP), BF16),
            dma((6,)),
            dma((10,)),
            dma((10,)),
            dma((10,)),
            dma((10,)),
            dma((4,)),
            dma((4,)),
        ],
        compiler_params=pltpu.CompilerParams(
            collective_id=0, has_side_effects=True, vmem_limit_bytes=48 * 1024 * 1024
        ),
    )(
        increment,
        diffusivity,
        sigma,
        tables,
        rinv.reshape(1, channels),
        innovation,
        obs_column,
        obs_table,
        obs_count,
    )


def solution(mesh):
    in_specs = (
        P(None, "lev", "band", None),
        P(None, "lev", "band", None),
        P(None, "lev", "band", None),
        P(None, None, None, "lev"),
        P(),
        P("band", None, None, None),
        P("band", None, None),
        P("band", None, None),
        P("band", None),
    )
    out_specs = P(None, "lev", "band", None)
    run = functools.partial(body, mesh.shape["band"], mesh.shape["lev"])
    return jax.shard_map(run, mesh=mesh, in_specs=in_specs, out_specs=out_specs, check_vma=False)
```

```python
import functools

import jax
import jax.numpy as jnp
from jax import lax
from jax.experimental import pallas as pl
from jax.experimental.pallas import tpu as pltpu
from jax.sharding import PartitionSpec as P

MESH = pl.DeviceIdType.MESH
F32 = jnp.float32
BF16 = jnp.bfloat16

NTAB = 4
STEPS = 3
HALO = 3
FIELDS = 2
LEV = 8
LON = 32
LAT = 128
CAP = 128
ROWS = LON + 8
EXT = LEV + 2 * HALO
WIDTH = FIELDS * LEV
PAIR = 2 * CAP


def dot(a, b, dims):
    return lax.dot_general(a, b, (dims, ((), ())), preferred_element_type=F32)


def run(step, work):
    work()


def kernel(
    nb,
    ng,
    inc_hbm,
    dif_hbm,
    sig_hbm,
    jac_hbm,
    rinv_hbm,
    inn_hbm,
    col_hbm,
    tab_hbm,
    cnt_hbm,
    out_hbm,
    out_v,
    inc_e,
    dif_e,
    sig_v,
    rinv_v,
    cnt_s,
    col_v,
    tab_v,
    inn_v,
    inn_f,
    inn_s,
    pack,
    lon_r,
    pack_w,
    lon_w,
    w_e,
    dfx,
    ua,
    ub,
    uc,
    st,
    s_mat,
    hot,
    a_mat,
    adj,
    prof,
    arr,
    junk,
    tabs,
    tabs_t,
    rcol,
    back,
    home,
    load_sem,
    halo_send,
    halo_recv,
    w_send,
    w_recv,
    tab_sem,
    x_sem,
):
    b, g = lax.axis_index("band"), lax.axis_index("lev")
    per = nb // ng
    nz = ng // 2
    z, core = g // 2, g % 2
    left, right = lax.rem(b + nb - 1, nb), lax.rem(b + 1, nb)
    hub = b // per
    has_low, has_high = g > 0, g < ng - 1
    channels = inn_v.shape[0]
    inn_rows = inn_v.shape[1]

    loads = [
        pltpu.make_async_copy(inc_hbm, inc_e.at[:, HALO : HALO + LEV], load_sem.at[0]),
        pltpu.make_async_copy(dif_hbm, dif_e.at[:, HALO : HALO + LEV], load_sem.at[1]),
        pltpu.make_async_copy(col_hbm.at[0], col_v, load_sem.at[2]),
        pltpu.make_async_copy(sig_hbm, sig_v, load_sem.at[3]),
        pltpu.make_async_copy(tab_hbm.at[0], tab_v, load_sem.at[4]),
        pltpu.make_async_copy(rinv_hbm, rinv_v, load_sem.at[5]),
        pltpu.make_async_copy(cnt_hbm, cnt_s, load_sem.at[6]),
        pltpu.make_async_copy(
            inn_hbm.at[
                0,
                :,
                pl.ds(pl.multiple_of((per * g) // inn_rows * inn_rows, inn_rows), inn_rows),
            ],
            inn_v,
            load_sem.at[7],
        ),
    ]
    l_inc, l_dif, l_col, l_sig, l_tab, l_rinv, l_cnt, l_inn = loads

    barrier = pltpu.get_barrier_semaphore()

    def greet(band, lev):
        pl.semaphore_signal(barrier, inc=1, device_id=(band, lev), device_id_type=MESH)

    def comm_greet():
        for side in (left, right):
            greet(side, g)
        for has, lev in ((has_low, g - 1), (has_high, g + 1)):

            @pl.when(has)
            def _():
                for side in (left, b, right):
                    greet(side, lev)

        @pl.loop(0, nz)
        def _(other):
            @pl.when(other != z)
            def _():
                greet(b, 2 * other + core)

        @pl.loop(0, per * ng)
        def _(index):
            band, lev = per * g + index // ng, index % ng

            @pl.when(jnp.logical_or(band != b, lev != g))
            def _():
                greet(band, lev)

    run(0, comm_greet)

    def start_loads():
        for load in loads:
            load.start()

    run(0, start_loads)

    zeros = jnp.zeros((FIELDS, HALO, LON, LAT), BF16)
    zeros_lon = jnp.zeros((2, HALO, 16, LAT), BF16)

    def clear():
        for edge, at in ((0, slice(0, HALO)), (ng - 1, slice(EXT - HALO, EXT))):

            @pl.when(g == edge)
            def _():
                inc_e[:, at] = zeros
                dif_e[:, at] = zeros
                w_e[:, at] = zeros
                lon_r[:, at] = zeros_lon
                lon_w[:, at] = zeros_lon

        for e in (0, EXT - 1):
            lon_r[:, e] = zeros_lon[:, 0]
            lon_w[:, e] = zeros_lon[:, 0]

    run(0, clear)

    sub = lax.broadcasted_iota(jnp.int32, (8, LAT), 0)
    upper = sub < 4

    def pack_level(l):
        for side in (0, 1):
            tiles = []
            for f in range(FIELDS):
                x = inc_e[f, HALO + l].astype(F32)
                d = dif_e[f, HALO + l].astype(F32)
                if side == 0:
                    tile = jnp.where(upper, x[0:8], pltpu.roll(d[0:8], 4, 0))
                else:
                    tile = jnp.where(upper, pltpu.roll(d[LON - 8 :], 4, 0), x[LON - 8 :])
                tiles.append(tile)
            pack[side, l] = jnp.concatenate(tiles, axis=0).astype(BF16)

    def packing():
        for l in range(LEV):
            pack_level(l)

    def wait_fields():
        l_inc.wait()
        l_dif.wait()

    run(0, wait_fields)
    run(0, packing)

    def comm_barrier():
        senders = (
            2
            + 3 * has_low.astype(jnp.int32)
            + 3 * has_high.astype(jnp.int32)
            + (nz - 1)
            + nb
            - (g == hub).astype(jnp.int32)
        )
        pl.semaphore_wait(barrier, senders)

    run(0, comm_barrier)

    def halo_copies(strips, lon_to, lev_pairs, send, recv):
        def copy(k, src, dst, band, lev):
            return pltpu.make_async_remote_copy(
                src_ref=src,
                dst_ref=dst,
                send_sem=send.at[k],
                recv_sem=recv.at[k],
                device_id=(band, lev),
                device_id_type=MESH,
            )

        level, up, down = [], [], []
        sides = (left, right)
        for i, (src, base, dst) in enumerate(lev_pairs):
            up.append(
                copy(6 + i, src.at[:, base + LEV - HALO : base + LEV], dst.at[:, 0:HALO], b, g + 1)
            )
            down.append(
                copy(8 + i, src.at[:, base : base + HALO], dst.at[:, EXT - HALO :], b, g - 1)
            )
        for k in (0, 1):
            level.append(copy(k, strips.at[k], lon_to.at[k, HALO : HALO + LEV], sides[k], g))
            up.append(copy(2 + k, strips.at[k, LEV - 2 :], lon_to.at[k, 1:HALO], sides[k], g + 1))
            down.append(
                copy(4 + k, strips.at[k, 0:2], lon_to.at[k, EXT - HALO : EXT - 1], sides[k], g - 1)
            )
        return level, up, down

    def halo_start(level, up, down):
        for c in level:
            c.start()
        for has, copies in ((has_high, up), (has_low, down)):

            @pl.when(has)
            def _():
                for c in copies:
                    c.start()

    def halo_arrive(level, up, down):
        for c in level:
            c.wait_recv()
        for has, copies in ((has_low, up), (has_high, down)):

            @pl.when(has)
            def _():
                for c in copies:
                    c.wait_recv()

    def halo_sent(level, up, down):
        for c in level:
            c.wait_send()
        for has, copies in ((has_high, up), (has_low, down)):

            @pl.when(has)
            def _():
                for c in copies:
                    c.wait_send()

    halo = halo_copies(
        pack, lon_r, ((inc_hbm, 0, inc_e), (dif_hbm, 0, dif_e)), halo_send, halo_recv
    )

    def comm_halo():
        halo_start(*halo)

    run(1, comm_halo)

    def comm_tabs():
        pltpu.make_async_copy(jac_hbm, tabs.at[core, z], tab_sem.at[1]).start()

        @pl.loop(0, nz)
        def _(other):
            @pl.when(other != z)
            def _():
                pltpu.make_async_remote_copy(
                    src_ref=jac_hbm,
                    dst_ref=tabs.at[core, z],
                    send_sem=tab_sem.at[0],
                    recv_sem=tab_sem.at[1],
                    device_id=(b, 2 * other + core),
                    device_id_type=MESH,
                ).start()

    run(5, comm_tabs)

    def col_row(i):
        return jnp.concatenate([col_v[pl.ds(2 * i, 1)], col_v[pl.ds(2 * i + 1, 1)]], axis=1)

    def lon_low(cols):
        return lax.shift_right_logical(cols, 7) & 15

    def build_hot(i):
        cols = col_row(i)
        want = (lax.shift_right_logical(cols, 11) & 1) * LAT + (cols & (LAT - 1))
        iota = lax.broadcasted_iota(jnp.int32, (2 * LAT, PAIR), 0)
        hot[:, pl.ds(pl.multiple_of(i * PAIR, PAIR), PAIR)] = jnp.where(
            iota == want, 1.0, 0.0
        ).astype(BF16)

    def make_hot():
        pl.loop(0, nb // 2)(build_hot)

    run(0, l_col.wait)
    run(2, make_hot)

    def comm_halo_arrive():
        halo_arrive(*halo)

    run(1, comm_halo_arrive)

    def widen_level(e):
        first = lon_r[0, e].astype(F32)
        last = lon_r[1, e].astype(F32)
        for f in range(FIELDS):
            r = first[8 * f : 8 * f + 8]
            l = last[8 * f : 8 * f + 8]
            ua[f, e, LON:] = jnp.where(upper, r, l)
            dfx[f, e, LON:] = pltpu.roll(jnp.where(upper, l, r), 4, 0)
            ua[f, e, 0:LON] = inc_e[f, e].astype(F32)
            dfx[f, e, 0:LON] = dif_e[f, e].astype(F32)

    def widen():
        pl.loop(0, EXT)(widen_level)

    run(3, widen)

    lane = lax.broadcasted_iota(jnp.int32, (ROWS, LAT), 1)

    def lap(ref, f, e):
        c = ref[f, e]
        total = ref[f, e - 1] + ref[f, e + 1]
        total = total + (pltpu.roll(c, 1, 0) + pltpu.roll(c, ROWS - 1, 0))
        total = total + jnp.where(lane == 0, 0.0, pltpu.roll(c, 1, 1))
        total = total + jnp.where(lane == LAT - 1, 0.0, pltpu.roll(c, LAT - 1, 1))
        return total - 6.0 * c

    def forward(src, dst, step):
        def body(e):
            for f in range(FIELDS):
                dst[f, e] = src[f, e] + dfx[f, e] * lap(src, f, e)

        pl.loop(step, EXT - step)(body)

    def last_step(l):
        for f in range(FIELDS):
            e = l + HALO
            field = (uc[f, e] + dfx[f, e] * lap(uc, f, e))[0:LON]
            st[pl.ds(pl.multiple_of((f * LEV + l) * LON, LON), LON)] = (
                sig_v[f, l].astype(F32) * field
            )

    def diffuse():
        forward(ua, ub, 1)
        forward(ub, uc, 2)
        pl.loop(0, LEV)(last_step)

    run(0, l_sig.wait)
    run(3, diffuse)

    def lay_out():
        for lon in range(LON):
            parts = [st[pl.ds(f * LEV * LON + lon, LEV, stride=LON)] for f in range(FIELDS)]
            s_mat[
                (lon % 16) * WIDTH : (lon % 16 + 1) * WIDTH,
                (lon // 16) * LAT : (lon // 16 + 1) * LAT,
            ] = jnp.concatenate(parts, axis=0).astype(BF16)

    run(4, lay_out)

    def pick(i):
        cols = col_row(i)
        low = lon_low(cols)
        chunk = hot[:, pl.ds(pl.multiple_of(i * PAIR, PAIR), PAIR)]
        rows = dot(s_mat[...], chunk, ((1,), (0,)))
        total = jnp.zeros((WIDTH, PAIR), F32)
        for k in range(16):
            total = jnp.where(low == k, rows[k * WIDTH : (k + 1) * WIDTH], total)
        total = total.astype(BF16)
        for half in range(2):
            prof[2 * i + half] = total[:, half * CAP : (half + 1) * CAP]

    def comm_profile(owner):
        here = jnp.logical_and(owner == b, g == hub)
        slot = arr.at[b % per, core, z]

        @pl.when(here)
        def _():
            pltpu.make_async_copy(prof.at[owner], slot, x_sem.at[1]).start()
            pltpu.make_async_copy(prof.at[owner], junk.at[0], x_sem.at[0]).start()

        @pl.when(jnp.logical_not(here))
        def _():
            pltpu.make_async_remote_copy(
                src_ref=prof.at[owner],
                dst_ref=slot,
                send_sem=x_sem.at[0],
                recv_sem=x_sem.at[1],
                device_id=(owner, hub),
                device_id_type=MESH,
            ).start()

    def gather():
        @pl.loop(0, nb // 2)
        def _(i):
            run(4, functools.partial(pick, i))
            for half in range(2):
                run(5, functools.partial(comm_profile, 2 * i + half))

    run(4, gather)

    share = pltpu.make_async_remote_copy(
        src_ref=tabs.at[core],
        dst_ref=tabs.at[core],
        send_sem=tab_sem.at[2],
        recv_sem=tab_sem.at[3],
        device_id=(b, g + 1 - 2 * core),
        device_id_type=MESH,
    )

    def comm_share():
        pltpu.make_async_copy(tabs.at[0], tabs.at[0], tab_sem.at[1]).wait()
        share.start()

    run(5, comm_share)

    def wait_rest():
        l_inn.wait()
        l_tab.wait()
        l_rinv.wait()
        l_cnt.wait()

    run(0, wait_rest)

    def spread_inn(i):
        at = pl.ds(pl.multiple_of(i * 8, 8), 8)
        inn_f[pl.ds(pl.multiple_of(i * 8 * inn_rows, 8 * inn_rows), 8 * inn_rows)] = (
            inn_v[at].astype(F32).reshape(8 * inn_rows, CAP)
        )

    def innovations():
        pl.loop(0, channels // 8)(spread_inn)
        row = lax.rem(per * g, inn_rows)
        for j in range(per):
            for i in range(channels // 8):
                inn_s[8 * i : 8 * i + 8, j * CAP : (j + 1) * CAP] = inn_f[
                    pl.ds(i * 8 * inn_rows + row + j, 8, stride=inn_rows)
                ]
        for i in range(channels // 128):
            line = rinv_v[:, i * 128 : (i + 1) * 128]
            rcol[i * 128 : (i + 1) * 128] = jnp.broadcast_to(line, (128, 128)).T

    run(6, innovations)

    def comm_tabs_arrive():
        pltpu.make_async_copy(tabs.at[0], tabs.at[0], tab_sem.at[3]).wait()

    run(5, comm_tabs_arrive)

    def table(t):
        return tabs[:, :, t].reshape(ng * WIDTH, channels)

    def turn_tables():
        for t in range(NTAB):
            tabs_t[t] = table(t).T

    run(6, turn_tables)

    def comm_arr():
        pltpu.make_async_copy(arr, arr, x_sem.at[1]).wait()

    run(5, comm_arr)

    def observe():
        profiles = jnp.concatenate(
            [arr[j].reshape(ng * WIDTH, CAP) for j in range(per)], axis=1
        )
        kinds = jnp.concatenate([tab_v[pl.ds(per * g + j, 1)] for j in range(per)], axis=1)
        slot_id = lax.broadcasted_iota(jnp.int32, (1, CAP), 1)
        valid = jnp.concatenate(
            [(slot_id < cnt_s[0, per * g + j]).astype(jnp.int32) for j in range(per)], axis=1
        )
        evolved = jnp.zeros((channels, per * CAP), F32)
        for t in range(NTAB):
            evolved = jnp.where(kinds == t, dot(tabs_t[t], profiles, ((1,), (0,))), evolved)
        scale = jnp.concatenate([rcol[...]] * per, axis=1)
        resid = jnp.where(valid > 0, scale * (evolved - inn_s[...]), 0.0)
        total = jnp.zeros((ng * WIDTH, per * CAP), F32)
        for t in range(NTAB):
            masked = jnp.where(kinds == t, resid, 0.0).astype(BF16)
            total = total + dot(table(t), masked, ((1,), (0,)))
        for j in range(per):
            back[j] = (
                total[:, j * CAP : (j + 1) * CAP].astype(BF16).reshape(2, nz, WIDTH, CAP)
            )

    run(7, observe)

    def comm_back():
        @pl.loop(0, per * ng)
        def _(index):
            j, lev = index // ng, index % ng
            band = per * g + j
            here = jnp.logical_and(band == b, lev == g)
            src = back.at[j, lev % 2, lev // 2]

            @pl.when(here)
            def _():
                pltpu.make_async_copy(src, home.at[b], x_sem.at[3]).start()
                pltpu.make_async_copy(src, junk.at[1], x_sem.at[2]).start()

            @pl.when(jnp.logical_not(here))
            def _():
                pltpu.make_async_remote_copy(
                    src_ref=src,
                    dst_ref=home.at[b],
                    send_sem=x_sem.at[2],
                    recv_sem=x_sem.at[3],
                    device_id=(band, lev),
                    device_id_type=MESH,
                ).start()

        pltpu.make_async_copy(home, home, x_sem.at[3]).wait()

    run(8, comm_back)

    def spread_home(i):
        low = lon_low(col_row(i))
        block = jnp.concatenate([home[2 * i], home[2 * i + 1]], axis=1).astype(F32)
        at = pl.ds(pl.multiple_of(i * PAIR, PAIR), PAIR)
        for k in range(16):
            a_mat[k * WIDTH : (k + 1) * WIDTH, at] = jnp.where(low == k, block, 0.0).astype(BF16)

    def spread():
        pl.loop(0, nb // 2)(spread_home)

    run(9, spread)

    def scatter():
        sums = dot(a_mat[...], hot[...], ((1,), (1,)))
        for k in range(2):
            adj[k * 256 : (k + 1) * 256] = sums[:, k * LAT : (k + 1) * LAT]

    run(9, scatter)

    def weigh():
        for l in range(LEV):
            firsts, lasts = [], []
            for f in range(FIELDS):
                for i in range(LON // 8):
                    cells = adj[pl.ds(i * 8 * WIDTH + f * LEV + l, 8, stride=WIDTH)]
                    w = sig_v[f, l, 8 * i : 8 * i + 8].astype(F32) * cells
                    ua[f, HALO + l, 8 * i : 8 * i + 8] = w
                    if i == 0:
                        firsts.append(w)
                    if i == LON // 8 - 1:
                        lasts.append(w)
            pack_w[0, l] = jnp.concatenate(firsts, axis=0).astype(BF16)
            pack_w[1, l] = jnp.concatenate(lasts, axis=0).astype(BF16)
            for f in range(FIELDS):
                w_e[f, HALO + l] = ua[f, HALO + l, 0:LON].astype(BF16)

    run(9, weigh)

    halo2 = halo_copies(pack_w, lon_w, ((w_e, HALO, w_e),), w_send, w_recv)

    def comm_halo2():
        halo_start(*halo2)
        halo_arrive(*halo2)

    run(10, comm_halo2)

    def widen_w():
        for e in range(EXT):
            first = lon_w[0, e].astype(F32)
            last = lon_w[1, e].astype(F32)
            for f in range(FIELDS):
                ua[f, e, LON:] = jnp.where(
                    upper, first[8 * f : 8 * f + 8], last[8 * f : 8 * f + 8]
                )
                if e < HALO or e >= HALO + LEV:
                    ua[f, e, 0:LON] = w_e[f, e].astype(F32)

    run(11, widen_w)

    def scale_level(e):
        for f in range(FIELDS):
            ub[f, e] = dfx[f, e] * ua[f, e]

    def backward(src, dst, step):
        def body(e):
            for f in range(FIELDS):
                w = ua[f, e] + lap(src, f, e)
                ua[f, e] = w
                dst[f, e] = dfx[f, e] * w

        pl.loop(step, EXT - step)(body)

    def finish(l):
        for f in range(FIELDS):
            e = l + HALO
            w = (ua[f, e] + lap(ub, f, e))[0:LON]
            out_v[f, l] = inc_e[f, e].astype(F32) + w

    def diffuse_back():
        pl.loop(0, EXT)(scale_level)
        backward(ub, uc, 1)
        backward(uc, ub, 2)
        pl.loop(0, LEV)(finish)

    run(11, diffuse_back)
    result = pltpu.make_async_copy(out_v, out_hbm, load_sem.at[8])
    result.start()

    def comm_gone():
        if nz > 1:
            gone = tabs.at[0, 0 : nz - 1]
            pltpu.make_async_copy(gone, gone, tab_sem.at[0]).wait()
        share.wait_send()
        pltpu.make_async_copy(prof, prof, x_sem.at[0]).wait()

    def comm_home_gone():
        pltpu.make_async_copy(back, back, x_sem.at[2]).wait()

    def comm_halo_gone():
        halo_sent(*halo)

    def comm_halo2_gone():
        halo_sent(*halo2)

    run(1, comm_halo_gone)
    run(5, comm_gone)
    run(8, comm_home_gone)
    run(10, comm_halo2_gone)
    result.wait()


def body(
    nb,
    ng,
    increment,
    diffusivity,
    sigma,
    jacobian,
    rinv,
    innovation,
    obs_column,
    obs_table,
    obs_count,
):
    channels = jacobian.shape[1]
    tables = jnp.transpose(jacobian, (0, 2, 3, 1)).reshape(NTAB, WIDTH, channels)
    per, nz = nb // ng, ng // 2
    hbm = pl.BlockSpec(memory_space=pltpu.HBM)
    dma = pltpu.SemaphoreType.DMA
    extended = pltpu.VMEM((FIELDS, EXT, LON, LAT), BF16)
    wide = pltpu.VMEM((FIELDS, EXT, ROWS, LAT), F32)
    return pl.pallas_call(
        functools.partial(kernel, nb, ng),
        out_shape=jax.ShapeDtypeStruct((FIELDS, LEV, LON, LAT), F32),
        in_specs=[hbm] * 9,
        out_specs=hbm,
        scratch_shapes=[
            pltpu.VMEM((FIELDS, LEV, LON, LAT), F32),
            extended,
            extended,
            pltpu.VMEM((FIELDS, LEV, LON, LAT), BF16),
            pltpu.VMEM((1, channels), F32),
            pltpu.SMEM((1, nb), jnp.int32),
            pltpu.VMEM((nb, CAP), jnp.int32),
            pltpu.VMEM((nb, CAP), jnp.int32),
            pltpu.VMEM((channels, min(16, nb), CAP), BF16),
            pltpu.VMEM((channels * min(16, nb), CAP), F32),
            pltpu.VMEM((channels, per * CAP), F32),
            pltpu.VMEM((2, LEV, 16, LAT), BF16),
            pltpu.VMEM((2, EXT, 16, LAT), BF16),
            pltpu.VMEM((2, LEV, 16, LAT), BF16),
            pltpu.VMEM((2, EXT, 16, LAT), BF16),
            extended,
            wide,
            wide,
            wide,
            wide,
            pltpu.VMEM((WIDTH * LON, LAT), F32),
            pltpu.VMEM((16 * WIDTH, 2 * LAT), BF16),
            pltpu.VMEM((2 * LAT, nb * CAP), BF16),
            pltpu.VMEM((16 * WIDTH, nb * CAP), BF16),
            pltpu.VMEM((WIDTH * LON, LAT), F32),
            pltpu.VMEM((nb, WIDTH, CAP), BF16),
            pltpu.VMEM((per, 2, nz, WIDTH, CAP), BF16),
            pltpu.VMEM((2, WIDTH, CAP), BF16),
            pltpu.VMEM((2, nz, NTAB, WIDTH, channels), BF16),
            pltpu.VMEM((NTAB, channels, ng * WIDTH), BF16),
            pltpu.VMEM((channels, CAP), F32),
            pltpu.VMEM((per, 2, nz, WIDTH, CAP), BF16),
            pltpu.VMEM((nb, WIDTH, CAP), BF16),
            dma((9,)),
            dma((10,)),
            dma((10,)),
            dma((10,)),
            dma((10,)),
            dma((4,)),
            dma((4,)),
        ],
        compiler_params=pltpu.CompilerParams(
            collective_id=0, has_side_effects=True, vmem_limit_bytes=60 * 1024 * 1024
        ),
    )(
        increment,
        diffusivity,
        sigma,
        tables,
        rinv.reshape(1, channels),
        innovation,
        obs_column,
        obs_table,
        obs_count,
    )


def solution(mesh):
    in_specs = (
        P(None, "lev", "band", None),
        P(None, "lev", "band", None),
        P(None, "lev", "band", None),
        P(None, None, None, "lev"),
        P(),
        P("band", None, None, None),
        P("band", None, None),
        P("band", None, None),
        P("band", None),
    )
    out_specs = P(None, "lev", "band", None)
    run = functools.partial(body, mesh.shape["band"], mesh.shape["lev"])
    return jax.shard_map(run, mesh=mesh, in_specs=in_specs, out_specs=out_specs, check_vma=False)
```

```python
import functools

import jax
import jax.numpy as jnp
from jax import lax
from jax.experimental import pallas as pl
from jax.experimental.pallas import tpu as pltpu
from jax.sharding import PartitionSpec as P

MESH = pl.DeviceIdType.MESH
F32 = jnp.float32
BF16 = jnp.bfloat16

NTAB = 4
STEPS = 3
HALO = 3
FIELDS = 2
LEV = 8
LON = 32
LAT = 128
CAP = 128
ROWS = LON + 8
EXT = LEV + 2 * HALO
WIDTH = FIELDS * LEV
PAIR = 2 * CAP


def dot(a, b, dims):
    return lax.dot_general(a, b, (dims, ((), ())), preferred_element_type=F32)


def run(step, work):
    work()


def kernel(
    nb,
    ng,
    inc_hbm,
    dif_hbm,
    sig_hbm,
    jac_hbm,
    rinv_hbm,
    inn_hbm,
    col_hbm,
    tab_hbm,
    cnt_hbm,
    out_hbm,
    out_v,
    inc_e,
    dif_e,
    sig_v,
    rinv_v,
    cnt_s,
    col_v,
    tab_v,
    inn_v,
    inn_f,
    inn_s,
    inn_r,
    pack,
    lon_r,
    pack_w,
    lon_w,
    w_e,
    dfx,
    ua,
    ub,
    uc,
    st,
    s_mat,
    hot,
    a_mat,
    adj,
    prof,
    arr,
    junk,
    tabs,
    tabs_t,
    rcol,
    back,
    home,
    load_sem,
    halo_send,
    halo_recv,
    w_send,
    w_recv,
    tab_sem,
    x_sem,
    swap_sem,
):
    b, g = lax.axis_index("band"), lax.axis_index("lev")
    nz = ng // 2
    z, core = g // 2, g % 2
    left, right = lax.rem(b + nb - 1, nb), lax.rem(b + 1, nb)
    mate = lax.rem(g + ng - lax.rem(b // 2, ng), ng)
    own_mate = mate == b // 2
    has_low, has_high = g > 0, g < ng - 1
    channels = inn_v.shape[0]
    inn_rows = inn_v.shape[1]

    loads = [
        pltpu.make_async_copy(inc_hbm, inc_e.at[:, HALO : HALO + LEV], load_sem.at[0]),
        pltpu.make_async_copy(dif_hbm, dif_e.at[:, HALO : HALO + LEV], load_sem.at[1]),
        pltpu.make_async_copy(col_hbm.at[0], col_v, load_sem.at[2]),
        pltpu.make_async_copy(sig_hbm, sig_v, load_sem.at[3]),
        pltpu.make_async_copy(tab_hbm.at[0], tab_v, load_sem.at[4]),
        pltpu.make_async_copy(rinv_hbm, rinv_v, load_sem.at[5]),
        pltpu.make_async_copy(cnt_hbm, cnt_s, load_sem.at[6]),
        pltpu.make_async_copy(
            inn_hbm.at[
                0,
                :,
                pl.ds(pl.multiple_of((2 * mate) // inn_rows * inn_rows, inn_rows), inn_rows),
            ],
            inn_v,
            load_sem.at[7],
        ),
    ]
    l_inc, l_dif, l_col, l_sig, l_tab, l_rinv, l_cnt, l_inn = loads

    barrier = pltpu.get_barrier_semaphore()

    def greet(band, lev):
        pl.semaphore_signal(barrier, inc=1, device_id=(band, lev), device_id_type=MESH)

    def comm_greet():
        for side in (left, right):
            greet(side, g)
        for has, lev in ((has_low, g - 1), (has_high, g + 1)):

            @pl.when(has)
            def _():
                for side in (left, right):
                    greet(side, lev)

        @pl.loop(1, ng)
        def _(i):
            greet(b, lax.rem(g + i, ng))

        for j in range(2):

            @pl.when(2 * mate + j != b)
            def _():
                greet(2 * mate + j, g)

    def start_loads():
        for load in loads:
            load.start()

    run(0, start_loads)
    run(0, comm_greet)

    zeros = jnp.zeros((FIELDS, HALO, LON, LAT), BF16)
    zeros_lon = jnp.zeros((2, HALO, 16, LAT), BF16)

    def clear():
        for edge, at in ((0, slice(0, HALO)), (ng - 1, slice(EXT - HALO, EXT))):

            @pl.when(g == edge)
            def _():
                inc_e[:, at] = zeros
                dif_e[:, at] = zeros
                w_e[:, at] = zeros
                lon_r[:, at] = zeros_lon
                lon_w[:, at] = zeros_lon

        for e in (0, EXT - 1):
            lon_r[:, e] = zeros_lon[:, 0]
            lon_w[:, e] = zeros_lon[:, 0]

    run(0, clear)

    sub = lax.broadcasted_iota(jnp.int32, (8, LAT), 0)
    upper = sub < 4

    def pack_level(l):
        for side in (0, 1):
            tiles = []
            for f in range(FIELDS):
                x = inc_e[f, HALO + l].astype(F32)
                d = dif_e[f, HALO + l].astype(F32)
                if side == 0:
                    tile = jnp.where(upper, x[0:8], pltpu.roll(d[0:8], 4, 0))
                else:
                    tile = jnp.where(upper, pltpu.roll(d[LON - 8 :], 4, 0), x[LON - 8 :])
                tiles.append(tile)
            pack[side, l] = jnp.concatenate(tiles, axis=0).astype(BF16)

    def packing():
        for l in range(LEV):
            pack_level(l)

    def wait_fields():
        l_inc.wait()
        l_dif.wait()

    run(0, wait_fields)
    run(0, packing)

    def comm_barrier():
        senders = (
            2
            + 2 * has_low.astype(jnp.int32)
            + 2 * has_high.astype(jnp.int32)
            + (ng - 1)
            + 2
            - own_mate.astype(jnp.int32)
        )
        pl.semaphore_wait(barrier, senders)

    run(0, comm_barrier)

    def halo_copies(strips, lon_to, lev_pairs, send, recv):
        def copy(k, src, dst, band, lev):
            return pltpu.make_async_remote_copy(
                src_ref=src,
                dst_ref=dst,
                send_sem=send.at[k],
                recv_sem=recv.at[k],
                device_id=(band, lev),
                device_id_type=MESH,
            )

        level, up, down = [], [], []
        sides = (left, right)
        for i, (src, base, dst) in enumerate(lev_pairs):
            up.append(
                copy(6 + i, src.at[:, base + LEV - HALO : base + LEV], dst.at[:, 0:HALO], b, g + 1)
            )
            down.append(
                copy(8 + i, src.at[:, base : base + HALO], dst.at[:, EXT - HALO :], b, g - 1)
            )
        for k in (0, 1):
            level.append(copy(k, strips.at[k], lon_to.at[k, HALO : HALO + LEV], sides[k], g))
            up.append(copy(2 + k, strips.at[k, LEV - 2 :], lon_to.at[k, 1:HALO], sides[k], g + 1))
            down.append(
                copy(4 + k, strips.at[k, 0:2], lon_to.at[k, EXT - HALO : EXT - 1], sides[k], g - 1)
            )
        return level, up, down

    def halo_start(level, up, down):
        for c in level:
            c.start()
        for has, copies in ((has_high, up), (has_low, down)):

            @pl.when(has)
            def _():
                for c in copies:
                    c.start()

    def halo_arrive(level, up, down):
        for c in level:
            c.wait_recv()
        for has, copies in ((has_low, up), (has_high, down)):

            @pl.when(has)
            def _():
                for c in copies:
                    c.wait_recv()

    def halo_sent(level, up, down):
        for c in level:
            c.wait_send()
        for has, copies in ((has_high, up), (has_low, down)):

            @pl.when(has)
            def _():
                for c in copies:
                    c.wait_send()

    halo = halo_copies(
        pack, lon_r, ((inc_hbm, 0, inc_e), (dif_hbm, 0, dif_e)), halo_send, halo_recv
    )

    def comm_halo():
        halo_start(*halo)

    run(1, comm_halo)

    def comm_tabs():
        pltpu.make_async_copy(jac_hbm, tabs.at[core, z], tab_sem.at[1]).start()

        @pl.loop(0, nz)
        def _(other):
            @pl.when(other != z)
            def _():
                pltpu.make_async_remote_copy(
                    src_ref=jac_hbm,
                    dst_ref=tabs.at[core, z],
                    send_sem=tab_sem.at[0],
                    recv_sem=tab_sem.at[1],
                    device_id=(b, 2 * other + core),
                    device_id_type=MESH,
                ).start()

    run(5, comm_tabs)

    def wait_observations():
        l_inn.wait()
        l_tab.wait()
        l_rinv.wait()
        l_cnt.wait()

    run(0, wait_observations)

    def spread_inn(i):
        at = pl.ds(pl.multiple_of(i * 8, 8), 8)
        inn_f[pl.ds(pl.multiple_of(i * 8 * inn_rows, 8 * inn_rows), 8 * inn_rows)] = (
            inn_v[at].astype(F32).reshape(8 * inn_rows, CAP)
        )

    def innovations():
        pl.loop(0, channels // 8)(spread_inn)
        row = lax.rem(2 * mate, inn_rows)
        slot_id = lax.broadcasted_iota(jnp.int32, (16, CAP), 1)
        for j in range(2):
            for i in range(channels // 16):
                halves = [
                    inn_f[pl.ds((2 * i + k) * 8 * inn_rows + row + j, 8, stride=inn_rows)]
                    for k in range(2)
                ]
                inn_s[j, 16 * i : 16 * i + 16] = jnp.concatenate(halves, axis=0).astype(BF16)
            kinds = jnp.broadcast_to(tab_v[pl.ds(2 * mate + j, 1)], (16, CAP))
            kinds = jnp.where(slot_id < cnt_s[0, 2 * mate + j], kinds, -1)
            inn_s[j, channels:] = kinds.astype(F32).astype(BF16)

    run(6, innovations)

    def swap_copy(j):
        return pltpu.make_async_remote_copy(
            src_ref=inn_s.at[j],
            dst_ref=inn_r.at[b % 2],
            send_sem=swap_sem.at[j],
            recv_sem=swap_sem.at[2],
            device_id=(2 * mate + j, g),
            device_id_type=MESH,
        )

    def comm_swap():
        for j in range(2):
            here = 2 * mate + j == b

            @pl.when(here)
            def _():
                pltpu.make_async_copy(inn_s.at[j], inn_r.at[b % 2], swap_sem.at[2]).start()

            @pl.when(jnp.logical_not(here))
            def _():
                swap_copy(j).start()

    def comm_swap_gone():
        for j in range(2):

            @pl.when(2 * mate + j != b)
            def _():
                swap_copy(j).wait_send()

    def comm_swap_arrive():
        pltpu.make_async_copy(inn_r, inn_r, swap_sem.at[2]).wait()

    run(5, comm_swap)

    def col_row(i):
        return jnp.concatenate([col_v[pl.ds(2 * i, 1)], col_v[pl.ds(2 * i + 1, 1)]], axis=1)

    def lon_low(cols):
        return lax.shift_right_logical(cols, 7) & 15

    def build_hot(i):
        cols = col_row(i)
        want = (lax.shift_right_logical(cols, 11) & 1) * LAT + (cols & (LAT - 1))
        iota = lax.broadcasted_iota(jnp.int32, (2 * LAT, PAIR), 0)
        hot[:, pl.ds(pl.multiple_of(i * PAIR, PAIR), PAIR)] = jnp.where(
            iota == want, 1.0, 0.0
        ).astype(BF16)

    def make_hot():
        pl.loop(0, nb // 2)(build_hot)

    run(0, l_col.wait)
    run(2, make_hot)

    def comm_halo_arrive():
        halo_arrive(*halo)

    run(1, comm_halo_arrive)

    def widen_level(e):
        first = lon_r[0, e].astype(F32)
        last = lon_r[1, e].astype(F32)
        for f in range(FIELDS):
            r = first[8 * f : 8 * f + 8]
            l = last[8 * f : 8 * f + 8]
            ua[f, e, LON:] = jnp.where(upper, r, l)
            dfx[f, e, LON:] = pltpu.roll(jnp.where(upper, l, r), 4, 0)
            ua[f, e, 0:LON] = inc_e[f, e].astype(F32)
            dfx[f, e, 0:LON] = dif_e[f, e].astype(F32)

    def widen():
        pl.loop(0, EXT)(widen_level)

    run(3, widen)

    lane = lax.broadcasted_iota(jnp.int32, (ROWS, LAT), 1)

    def lap(ref, f, e):
        c = ref[f, e]
        total = ref[f, e - 1] + ref[f, e + 1]
        total = total + (pltpu.roll(c, 1, 0) + pltpu.roll(c, ROWS - 1, 0))
        total = total + jnp.where(lane == 0, 0.0, pltpu.roll(c, 1, 1))
        total = total + jnp.where(lane == LAT - 1, 0.0, pltpu.roll(c, LAT - 1, 1))
        return total - 6.0 * c

    def forward(src, dst, step):
        def body(e):
            for f in range(FIELDS):
                dst[f, e] = src[f, e] + dfx[f, e] * lap(src, f, e)

        pl.loop(step, EXT - step)(body)

    def last_step(l):
        for f in range(FIELDS):
            e = l + HALO
            field = (uc[f, e] + dfx[f, e] * lap(uc, f, e))[0:LON]
            st[pl.ds(pl.multiple_of((f * LEV + l) * LON, LON), LON)] = (
                sig_v[f, l].astype(F32) * field
            )

    def diffuse():
        forward(ua, ub, 1)
        forward(ub, uc, 2)
        pl.loop(0, LEV)(last_step)

    run(0, l_sig.wait)
    run(3, diffuse)

    def lay_out():
        for lon in range(LON):
            parts = [st[pl.ds(f * LEV * LON + lon, LEV, stride=LON)] for f in range(FIELDS)]
            s_mat[
                (lon % 16) * WIDTH : (lon % 16 + 1) * WIDTH,
                (lon // 16) * LAT : (lon // 16 + 1) * LAT,
            ] = jnp.concatenate(parts, axis=0).astype(BF16)

    run(4, lay_out)

    def pick(i):
        cols = col_row(i)
        low = lon_low(cols)
        chunk = hot[:, pl.ds(pl.multiple_of(i * PAIR, PAIR), PAIR)]
        rows = dot(s_mat[...], chunk, ((1,), (0,)))
        total = jnp.zeros((WIDTH, PAIR), F32)
        for k in range(16):
            total = jnp.where(low == k, rows[k * WIDTH : (k + 1) * WIDTH], total)
        prof[i] = total.astype(BF16)

    def comm_profile(i, lev):
        pltpu.make_async_remote_copy(
            src_ref=prof.at[i],
            dst_ref=arr.at[core, z],
            send_sem=x_sem.at[0],
            recv_sem=x_sem.at[1],
            device_id=(b, lev),
            device_id_type=MESH,
        ).start()

    def comm_profile_own(i):
        pltpu.make_async_copy(prof.at[i], arr.at[core, z], x_sem.at[1]).start()
        pltpu.make_async_copy(prof.at[i], junk.at[0], x_sem.at[0]).start()

    hops = sorted(range(nz), key=lambda d: -min(d, nz - d))
    order = [(d, c) for d in hops for c in (0, 1) if (d, c) != (0, 0)] + [(0, 0)]

    def gather():
        for d, c in order:
            lev = 2 * lax.rem(z + d, nz) + (core + c) % 2
            i = lax.rem(lev + ng - lax.rem(b // 2, ng), ng)
            run(4, functools.partial(pick, i))
            if (d, c) == (0, 0):
                run(5, functools.partial(comm_profile_own, i))
            else:
                run(5, functools.partial(comm_profile, i, lev))

    run(4, gather)

    share = pltpu.make_async_remote_copy(
        src_ref=tabs.at[core],
        dst_ref=tabs.at[core],
        send_sem=tab_sem.at[2],
        recv_sem=tab_sem.at[3],
        device_id=(b, g + 1 - 2 * core),
        device_id_type=MESH,
    )

    def comm_share():
        pltpu.make_async_copy(tabs.at[0], tabs.at[0], tab_sem.at[1]).wait()
        share.start()

    run(5, comm_share)

    def turn_rinv():
        for i in range(channels // 128):
            line = rinv_v[:, i * 128 : (i + 1) * 128]
            rcol[i * 128 : (i + 1) * 128] = jnp.broadcast_to(line, (128, 128)).T

    run(6, turn_rinv)

    def comm_tabs_arrive():
        pltpu.make_async_copy(tabs.at[0], tabs.at[0], tab_sem.at[3]).wait()

    run(5, comm_tabs_arrive)

    def table(t):
        return tabs[:, :, t].reshape(ng * WIDTH, channels)

    def turn_tables():
        for t in range(NTAB):
            tabs_t[t] = table(t).T

    run(6, turn_tables)

    def comm_arr():
        pltpu.make_async_copy(arr, arr, x_sem.at[1]).wait()

    run(5, comm_arr)

    def observe():
        profiles = arr[...].reshape(ng * WIDTH, PAIR)
        kinds = jnp.concatenate(
            [inn_r[j, channels:].astype(F32)[0:1] for j in range(2)], axis=1
        )
        seen = jnp.concatenate([inn_r[j, 0:channels].astype(F32) for j in range(2)], axis=1)
        evolved = jnp.zeros((channels, PAIR), F32)
        for t in range(NTAB):
            evolved = jnp.where(kinds == t, dot(tabs_t[t], profiles, ((1,), (0,))), evolved)
        scale = jnp.concatenate([rcol[...]] * 2, axis=1)
        resid = scale * (evolved - seen)
        total = jnp.zeros((ng * WIDTH, PAIR), F32)
        for t in range(NTAB):
            masked = jnp.where(kinds == t, resid, 0.0).astype(BF16)
            total = total + dot(table(t), masked, ((1,), (0,)))
        back[...] = total.astype(BF16).reshape(2, nz, WIDTH, PAIR)

    run(5, comm_swap_arrive)
    run(7, observe)

    def comm_back():
        for d, c in order:
            oz, oc = lax.rem(z + d, nz), (core + c) % 2
            src = back.at[oc, oz]
            if (d, c) == (0, 0):
                pltpu.make_async_copy(src, home.at[mate], x_sem.at[3]).start()
                pltpu.make_async_copy(src, junk.at[1], x_sem.at[2]).start()
            else:
                pltpu.make_async_remote_copy(
                    src_ref=src,
                    dst_ref=home.at[mate],
                    send_sem=x_sem.at[2],
                    recv_sem=x_sem.at[3],
                    device_id=(b, 2 * oz + oc),
                    device_id_type=MESH,
                ).start()
        pltpu.make_async_copy(home, home, x_sem.at[3]).wait()

    run(8, comm_back)

    def spread_home(i):
        low = lon_low(col_row(i))
        block = home[i].astype(F32)
        at = pl.ds(pl.multiple_of(i * PAIR, PAIR), PAIR)
        for k in range(16):
            a_mat[k * WIDTH : (k + 1) * WIDTH, at] = jnp.where(low == k, block, 0.0).astype(BF16)

    def spread():
        pl.loop(0, nb // 2)(spread_home)

    run(9, spread)

    def scatter():
        sums = dot(a_mat[...], hot[...], ((1,), (1,)))
        for k in range(2):
            adj[k * 256 : (k + 1) * 256] = sums[:, k * LAT : (k + 1) * LAT]

    run(9, scatter)

    def weigh():
        for l in range(LEV):
            firsts, lasts = [], []
            for f in range(FIELDS):
                for i in range(LON // 8):
                    cells = adj[pl.ds(i * 8 * WIDTH + f * LEV + l, 8, stride=WIDTH)]
                    w = sig_v[f, l, 8 * i : 8 * i + 8].astype(F32) * cells
                    ua[f, HALO + l, 8 * i : 8 * i + 8] = w
                    if i == 0:
                        firsts.append(w)
                    if i == LON // 8 - 1:
                        lasts.append(w)
            pack_w[0, l] = jnp.concatenate(firsts, axis=0).astype(BF16)
            pack_w[1, l] = jnp.concatenate(lasts, axis=0).astype(BF16)
            for f in range(FIELDS):
                w_e[f, HALO + l] = ua[f, HALO + l, 0:LON].astype(BF16)

    run(9, weigh)

    halo2 = halo_copies(pack_w, lon_w, ((w_e, HALO, w_e),), w_send, w_recv)

    def comm_halo2():
        halo_start(*halo2)
        halo_arrive(*halo2)

    run(10, comm_halo2)

    def widen_w():
        for e in range(EXT):
            first = lon_w[0, e].astype(F32)
            last = lon_w[1, e].astype(F32)
            for f in range(FIELDS):
                ua[f, e, LON:] = jnp.where(
                    upper, first[8 * f : 8 * f + 8], last[8 * f : 8 * f + 8]
                )
                if e < HALO or e >= HALO + LEV:
                    ua[f, e, 0:LON] = w_e[f, e].astype(F32)

    run(11, widen_w)

    def scale_level(e):
        for f in range(FIELDS):
            ub[f, e] = dfx[f, e] * ua[f, e]

    def backward(src, dst, step):
        def body(e):
            for f in range(FIELDS):
                w = ua[f, e] + lap(src, f, e)
                ua[f, e] = w
                dst[f, e] = dfx[f, e] * w

        pl.loop(step, EXT - step)(body)

    def finish(l):
        for f in range(FIELDS):
            e = l + HALO
            w = (ua[f, e] + lap(ub, f, e))[0:LON]
            out_v[f, l] = inc_e[f, e].astype(F32) + w

    def diffuse_back():
        pl.loop(0, EXT)(scale_level)
        backward(ub, uc, 1)
        backward(uc, ub, 2)
        pl.loop(0, LEV)(finish)

    run(11, diffuse_back)
    result = pltpu.make_async_copy(out_v, out_hbm, load_sem.at[8])
    result.start()

    def comm_gone():
        if nz > 1:
            gone = tabs.at[0, 0 : nz - 1]
            pltpu.make_async_copy(gone, gone, tab_sem.at[0]).wait()
        share.wait_send()
        pltpu.make_async_copy(prof, prof, x_sem.at[0]).wait()

    def comm_home_gone():
        pltpu.make_async_copy(back, back, x_sem.at[2]).wait()

    def comm_halo_gone():
        halo_sent(*halo)

    def comm_halo2_gone():
        halo_sent(*halo2)

    run(1, comm_halo_gone)
    run(5, comm_swap_gone)
    run(5, comm_gone)
    run(8, comm_home_gone)
    run(10, comm_halo2_gone)
    result.wait()


def body(
    nb,
    ng,
    increment,
    diffusivity,
    sigma,
    jacobian,
    rinv,
    innovation,
    obs_column,
    obs_table,
    obs_count,
):
    channels = jacobian.shape[1]
    tables = jnp.transpose(jacobian, (0, 2, 3, 1)).reshape(NTAB, WIDTH, channels)
    nz = ng // 2
    hbm = pl.BlockSpec(memory_space=pltpu.HBM)
    dma = pltpu.SemaphoreType.DMA
    extended = pltpu.VMEM((FIELDS, EXT, LON, LAT), BF16)
    wide = pltpu.VMEM((FIELDS, EXT, ROWS, LAT), F32)
    return pl.pallas_call(
        functools.partial(kernel, nb, ng),
        out_shape=jax.ShapeDtypeStruct((FIELDS, LEV, LON, LAT), F32),
        in_specs=[hbm] * 9,
        out_specs=hbm,
        scratch_shapes=[
            pltpu.VMEM((FIELDS, LEV, LON, LAT), F32),
            extended,
            extended,
            pltpu.VMEM((FIELDS, LEV, LON, LAT), BF16),
            pltpu.VMEM((1, channels), F32),
            pltpu.SMEM((1, nb), jnp.int32),
            pltpu.VMEM((nb, CAP), jnp.int32),
            pltpu.VMEM((nb, CAP), jnp.int32),
            pltpu.VMEM((channels, min(16, nb), CAP), BF16),
            pltpu.VMEM((channels * min(16, nb), CAP), F32),
            pltpu.VMEM((2, channels + 16, CAP), BF16),
            pltpu.VMEM((2, channels + 16, CAP), BF16),
            pltpu.VMEM((2, LEV, 16, LAT), BF16),
            pltpu.VMEM((2, EXT, 16, LAT), BF16),
            pltpu.VMEM((2, LEV, 16, LAT), BF16),
            pltpu.VMEM((2, EXT, 16, LAT), BF16),
            extended,
            wide,
            wide,
            wide,
            wide,
            pltpu.VMEM((WIDTH * LON, LAT), F32),
            pltpu.VMEM((16 * WIDTH, 2 * LAT), BF16),
            pltpu.VMEM((2 * LAT, nb * CAP), BF16),
            pltpu.VMEM((16 * WIDTH, nb * CAP), BF16),
            pltpu.VMEM((WIDTH * LON, LAT), F32),
            pltpu.VMEM((ng, WIDTH, PAIR), BF16),
            pltpu.VMEM((2, nz, WIDTH, PAIR), BF16),
            pltpu.VMEM((2, WIDTH, PAIR), BF16),
            pltpu.VMEM((2, nz, NTAB, WIDTH, channels), BF16),
            pltpu.VMEM((NTAB, channels, ng * WIDTH), BF16),
            pltpu.VMEM((channels, CAP), F32),
            pltpu.VMEM((2, nz, WIDTH, PAIR), BF16),
            pltpu.VMEM((ng, WIDTH, PAIR), BF16),
            dma((9,)),
            dma((10,)),
            dma((10,)),
            dma((10,)),
            dma((10,)),
            dma((4,)),
            dma((4,)),
            dma((3,)),
        ],
        compiler_params=pltpu.CompilerParams(
            collective_id=0, has_side_effects=True, vmem_limit_bytes=60 * 1024 * 1024
        ),
    )(
        increment,
        diffusivity,
        sigma,
        tables,
        rinv.reshape(1, channels),
        innovation,
        obs_column,
        obs_table,
        obs_count,
    )


def solution(mesh):
    in_specs = (
        P(None, "lev", "band", None),
        P(None, "lev", "band", None),
        P(None, "lev", "band", None),
        P(None, None, None, "lev"),
        P(),
        P("band", None, None, None),
        P("band", None, None),
        P("band", None, None),
        P("band", None),
    )
    out_specs = P(None, "lev", "band", None)
    run = functools.partial(body, mesh.shape["band"], mesh.shape["lev"])
    return jax.shard_map(run, mesh=mesh, in_specs=in_specs, out_specs=out_specs, check_vma=False)
```

```python
import functools

import jax
import jax.numpy as jnp
from jax import lax
from jax.experimental import pallas as pl
from jax.experimental.pallas import tpu as pltpu
from jax.sharding import PartitionSpec as P

MESH = pl.DeviceIdType.MESH
F32 = jnp.float32
BF16 = jnp.bfloat16

NTAB = 4
STEPS = 3
HALO = 3
FIELDS = 2
LEV = 8
LON = 32
LAT = 128
CAP = 128
ROWS = LON + 8
EXT = LEV + 2 * HALO
WIDTH = FIELDS * LEV
PAIR = 2 * CAP


def dot(a, b, dims):
    return lax.dot_general(a, b, (dims, ((), ())), preferred_element_type=F32)


def gap(lev, ng):
    rank = ng - 1 - lev
    if ng != 16:
        return 0, rank, 1, ng
    long, short = rank // 4, rank % 4
    turn = lambda k: k + (k >= 2).astype(jnp.int32) - 2 * (k >= 3).astype(jnp.int32)
    return turn(short), turn(long), 4, 4


def pair_on(pair, lev, ng, sign):
    dx, dy, nx, ny = gap(lev, ng)
    x = lax.rem(pair // ny + nx + sign * dx, nx)
    y = lax.rem(pair % ny + ny + sign * dy, ny)
    return x * ny + y


def run(step, work):
    work()


def kernel(
    nb,
    ng,
    inc_hbm,
    dif_hbm,
    sig_hbm,
    jac_hbm,
    rinv_hbm,
    inn_hbm,
    col_hbm,
    tab_hbm,
    cnt_hbm,
    out_hbm,
    out_v,
    inc_e,
    dif_e,
    sig_v,
    rinv_v,
    cnt_s,
    col_v,
    tab_v,
    inn_v,
    inn_f,
    inn_s,
    inn_r,
    pack,
    lon_r,
    pack_w,
    lon_w,
    w_e,
    dfx,
    ua,
    ub,
    uc,
    st,
    s_mat,
    hot,
    a_mat,
    adj,
    prof,
    arr,
    junk,
    tabs,
    tabs_t,
    rcol,
    back,
    home,
    load_sem,
    halo_send,
    halo_recv,
    w_send,
    w_recv,
    tab_sem,
    x_sem,
    swap_sem,
):
    b, g = lax.axis_index("band"), lax.axis_index("lev")
    nz = ng // 2
    z, core = g // 2, g % 2
    left, right = lax.rem(b + nb - 1, nb), lax.rem(b + 1, nb)
    to_pair = pair_on(b // 2, g, ng, 1)
    from_pair = pair_on(b // 2, g, ng, -1)
    own_pair = to_pair == b // 2
    has_low, has_high = g > 0, g < ng - 1
    channels = inn_v.shape[0]
    inn_rows = inn_v.shape[1]

    hops = sorted(range(nz), key=lambda d: -min(d, nz - d))
    order = [(d, c) for d in hops for c in (0, 1) if (d, c) != (0, 0)] + [(0, 0)]

    loads = [
        pltpu.make_async_copy(inc_hbm, inc_e.at[:, HALO : HALO + LEV], load_sem.at[0]),
        pltpu.make_async_copy(dif_hbm, dif_e.at[:, HALO : HALO + LEV], load_sem.at[1]),
        pltpu.make_async_copy(col_hbm.at[0], col_v, load_sem.at[2]),
        pltpu.make_async_copy(sig_hbm, sig_v, load_sem.at[3]),
        pltpu.make_async_copy(tab_hbm.at[0], tab_v, load_sem.at[4]),
        pltpu.make_async_copy(rinv_hbm, rinv_v, load_sem.at[5]),
        pltpu.make_async_copy(cnt_hbm, cnt_s, load_sem.at[6]),
        pltpu.make_async_copy(
            inn_hbm.at[
                0,
                :,
                pl.ds(pl.multiple_of((2 * to_pair) // inn_rows * inn_rows, inn_rows), inn_rows),
            ],
            inn_v,
            load_sem.at[7],
        ),
    ]
    l_inc, l_dif, l_col, l_sig, l_tab, l_rinv, l_cnt, l_inn = loads

    barrier = pltpu.get_barrier_semaphore()

    def greet(band, lev):
        pl.semaphore_signal(barrier, inc=1, device_id=(band, lev), device_id_type=MESH)

    def comm_greet():
        for d, c in order[:-1]:
            greet(b, 2 * lax.rem(z + d, nz) + (core + c) % 2)
        for j in range(2):

            @pl.when(2 * from_pair + j != b)
            def _():
                greet(2 * from_pair + j, g)

        for has, lev in ((has_low, g - 1), (has_high, g + 1)):

            @pl.when(has)
            def _():
                for side in (left, right):
                    greet(side, lev)

        for side in (left, right):
            greet(side, g)

    def start_loads():
        for load in loads:
            load.start()

    run(0, comm_greet)
    run(0, start_loads)

    zeros = jnp.zeros((FIELDS, HALO, LON, LAT), BF16)
    zeros_lon = jnp.zeros((2, HALO, 16, LAT), BF16)

    def clear():
        for edge, at in ((0, slice(0, HALO)), (ng - 1, slice(EXT - HALO, EXT))):

            @pl.when(g == edge)
            def _():
                inc_e[:, at] = zeros
                dif_e[:, at] = zeros
                w_e[:, at] = zeros
                lon_r[:, at] = zeros_lon
                lon_w[:, 0 if edge == 0 else LEV // 2 + 1] = zeros_lon[:, 0]

        for e in (0, EXT - 1):
            lon_r[:, e] = zeros_lon[:, 0]
            for f in range(FIELDS):
                ua[f, e, LON:] = jnp.zeros((8, LAT), F32)

    run(0, clear)

    sub = lax.broadcasted_iota(jnp.int32, (8, LAT), 0)
    upper = sub < 4

    def pack_level(l):
        for side in (0, 1):
            tiles = []
            for f in range(FIELDS):
                x = inc_e[f, HALO + l].astype(F32)
                d = dif_e[f, HALO + l].astype(F32)
                if side == 0:
                    tile = jnp.where(upper, x[0:8], pltpu.roll(d[0:8], 4, 0))
                else:
                    tile = jnp.where(upper, pltpu.roll(d[LON - 8 :], 4, 0), x[LON - 8 :])
                tiles.append(tile)
            pack[side, l] = jnp.concatenate(tiles, axis=0).astype(BF16)

    def packing():
        for l in range(LEV):
            pack_level(l)

    def wait_fields():
        l_inc.wait()
        l_dif.wait()

    run(0, wait_fields)
    run(0, packing)

    def comm_barrier():
        senders = (
            2
            + 2 * has_low.astype(jnp.int32)
            + 2 * has_high.astype(jnp.int32)
            + (ng - 1)
            + 2
            - own_pair.astype(jnp.int32)
        )
        pl.semaphore_wait(barrier, senders)

    run(0, comm_barrier)

    def halo_copies(strips, lon_to, lev_pairs, send, recv):
        def copy(k, src, dst, band, lev):
            return pltpu.make_async_remote_copy(
                src_ref=src,
                dst_ref=dst,
                send_sem=send.at[k],
                recv_sem=recv.at[k],
                device_id=(band, lev),
                device_id_type=MESH,
            )

        level, up, down = [], [], []
        sides = (left, right)
        count = strips.shape[1]
        edge = 2 * count // LEV
        base = (lon_to.shape[1] - count) // 2
        for k in (0, 1):
            level.append(copy(k, strips.at[k], lon_to.at[k, base : base + count], sides[k], g))
            up.append(
                copy(2 + k, strips.at[k, count - edge :], lon_to.at[k, base - edge : base], sides[k], g + 1)
            )
            down.append(
                copy(
                    4 + k,
                    strips.at[k, 0:edge],
                    lon_to.at[k, base + count : base + count + edge],
                    sides[k],
                    g - 1,
                )
            )
        for i, (src, first, dst) in enumerate(lev_pairs):
            up.append(
                copy(6 + i, src.at[:, first + LEV - HALO : first + LEV], dst.at[:, 0:HALO], b, g + 1)
            )
            down.append(
                copy(8 + i, src.at[:, first : first + HALO], dst.at[:, EXT - HALO :], b, g - 1)
            )
        return level, up, down

    def halo_start(level, up, down):
        for part in (slice(0, 2), slice(2, None)):
            for has, copies in ((has_high, up), (has_low, down)):

                @pl.when(has)
                def _():
                    for c in copies[part]:
                        c.start()

            if part.start == 0:
                for c in level:
                    c.start()

    def halo_arrive(level, up, down):
        for c in level:
            c.wait_recv()
        for has, copies in ((has_low, up), (has_high, down)):

            @pl.when(has)
            def _():
                for c in copies:
                    c.wait_recv()

    def halo_sent(level, up, down):
        for c in level:
            c.wait_send()
        for has, copies in ((has_high, up), (has_low, down)):

            @pl.when(has)
            def _():
                for c in copies:
                    c.wait_send()

    halo = halo_copies(
        pack, lon_r, ((inc_hbm, 0, inc_e), (dif_hbm, 0, dif_e)), halo_send, halo_recv
    )

    def comm_halo():
        halo_start(*halo)

    run(1, comm_halo)

    def comm_tabs():
        pltpu.make_async_copy(jac_hbm, tabs.at[core, z], tab_sem.at[1]).start()

        for d in hops[:-1]:
            pltpu.make_async_remote_copy(
                src_ref=jac_hbm,
                dst_ref=tabs.at[core, z],
                send_sem=tab_sem.at[0],
                recv_sem=tab_sem.at[1],
                device_id=(b, 2 * lax.rem(z + d, nz) + core),
                device_id_type=MESH,
            ).start()

    run(5, comm_tabs)

    def wait_observations():
        l_inn.wait()
        l_tab.wait()
        l_rinv.wait()
        l_cnt.wait()

    run(0, wait_observations)

    def spread_inn(i):
        at = pl.ds(pl.multiple_of(i * 8, 8), 8)
        inn_f[pl.ds(pl.multiple_of(i * 8 * inn_rows, 8 * inn_rows), 8 * inn_rows)] = (
            inn_v[at].astype(F32).reshape(8 * inn_rows, CAP)
        )

    def innovations():
        pl.loop(0, channels // 8)(spread_inn)
        row = lax.rem(2 * to_pair, inn_rows)
        slot_id = lax.broadcasted_iota(jnp.int32, (16, CAP), 1)
        for j in range(2):
            for i in range(channels // 16):
                halves = [
                    inn_f[pl.ds((2 * i + k) * 8 * inn_rows + row + j, 8, stride=inn_rows)]
                    for k in range(2)
                ]
                inn_s[j, 16 * i : 16 * i + 16] = jnp.concatenate(halves, axis=0).astype(BF16)
            kinds = jnp.broadcast_to(tab_v[pl.ds(2 * to_pair + j, 1)], (16, CAP))
            kinds = jnp.where(slot_id < cnt_s[0, 2 * to_pair + j], kinds, -1)
            inn_s[j, channels:] = kinds.astype(F32).astype(BF16)

    run(6, innovations)

    def swap_copy(j):
        return pltpu.make_async_remote_copy(
            src_ref=inn_s.at[j],
            dst_ref=inn_r.at[b % 2],
            send_sem=swap_sem.at[j],
            recv_sem=swap_sem.at[2],
            device_id=(2 * to_pair + j, g),
            device_id_type=MESH,
        )

    def comm_swap():
        for j in range(2):
            here = 2 * to_pair + j == b

            @pl.when(here)
            def _():
                pltpu.make_async_copy(inn_s.at[j], inn_r.at[b % 2], swap_sem.at[2]).start()

            @pl.when(jnp.logical_not(here))
            def _():
                swap_copy(j).start()

    def comm_swap_gone():
        for j in range(2):

            @pl.when(2 * to_pair + j != b)
            def _():
                swap_copy(j).wait_send()

    def comm_swap_arrive():
        pltpu.make_async_copy(inn_r, inn_r, swap_sem.at[2]).wait()

    run(5, comm_swap)

    def col_row(i):
        return jnp.concatenate([col_v[pl.ds(2 * i, 1)], col_v[pl.ds(2 * i + 1, 1)]], axis=1)

    def lon_low(cols):
        return lax.shift_right_logical(cols, 7) & 15

    def build_hot(i):
        cols = col_row(i)
        want = (lax.shift_right_logical(cols, 11) & 1) * LAT + (cols & (LAT - 1))
        iota = lax.broadcasted_iota(jnp.int32, (2 * LAT, PAIR), 0)
        hot[:, pl.ds(pl.multiple_of(i * PAIR, PAIR), PAIR)] = jnp.where(
            iota == want, 1.0, 0.0
        ).astype(BF16)

    def make_hot():
        pl.loop(0, nb // 2)(build_hot)

    run(0, l_col.wait)
    run(2, make_hot)

    def comm_halo_arrive():
        halo_arrive(*halo)

    run(1, comm_halo_arrive)

    def widen_level(e):
        first = lon_r[0, e].astype(F32)
        last = lon_r[1, e].astype(F32)
        for f in range(FIELDS):
            r = first[8 * f : 8 * f + 8]
            l = last[8 * f : 8 * f + 8]
            ua[f, e, LON:] = jnp.where(upper, r, l)
            dfx[f, e, LON:] = pltpu.roll(jnp.where(upper, l, r), 4, 0)
            ua[f, e, 0:LON] = inc_e[f, e].astype(F32)
            dfx[f, e, 0:LON] = dif_e[f, e].astype(F32)

    def widen():
        for e in range(EXT):
            widen_level(e)

    run(3, widen)

    lane = lax.broadcasted_iota(jnp.int32, (ROWS, LAT), 1)

    def lap(ref, f, e):
        c = ref[f, e]
        total = ref[f, e - 1] + ref[f, e + 1]
        total = total + (pltpu.roll(c, 1, 0) + pltpu.roll(c, ROWS - 1, 0))
        total = total + jnp.where(lane == 0, 0.0, pltpu.roll(c, 1, 1))
        total = total + jnp.where(lane == LAT - 1, 0.0, pltpu.roll(c, LAT - 1, 1))
        return total - 6.0 * c

    def forward(src, dst, step):
        for e in range(step, EXT - step):
            for f in range(FIELDS):
                dst[f, e] = src[f, e] + dfx[f, e] * lap(src, f, e)

    def last_step(l):
        for f in range(FIELDS):
            e = l + HALO
            field = (uc[f, e] + dfx[f, e] * lap(uc, f, e))[0:LON]
            st[(f * LEV + l) * LON : (f * LEV + l + 1) * LON] = (
                sig_v[f, l].astype(F32) * field
            )

    def diffuse():
        forward(ua, ub, 1)
        forward(ub, uc, 2)
        for l in range(LEV):
            last_step(l)

    run(0, l_sig.wait)
    run(3, diffuse)

    def lay_out():
        for lon in range(LON):
            parts = [st[pl.ds(f * LEV * LON + lon, LEV, stride=LON)] for f in range(FIELDS)]
            s_mat[
                (lon % 16) * WIDTH : (lon % 16 + 1) * WIDTH,
                (lon // 16) * LAT : (lon // 16 + 1) * LAT,
            ] = jnp.concatenate(parts, axis=0).astype(BF16)

    run(4, lay_out)

    def pick(i):
        cols = col_row(i)
        low = lon_low(cols)
        chunk = hot[:, pl.ds(pl.multiple_of(i * PAIR, PAIR), PAIR)]
        rows = dot(s_mat[...], chunk, ((1,), (0,)))
        total = jnp.zeros((WIDTH, PAIR), F32)
        for k in range(16):
            total = jnp.where(low == k, rows[k * WIDTH : (k + 1) * WIDTH], total)
        prof[i] = total.astype(BF16)

    def comm_profile(i, lev):
        pltpu.make_async_remote_copy(
            src_ref=prof.at[i],
            dst_ref=arr.at[core, z],
            send_sem=x_sem.at[0],
            recv_sem=x_sem.at[1],
            device_id=(b, lev),
            device_id_type=MESH,
        ).start()

    def comm_profile_own(i):
        pltpu.make_async_copy(prof.at[i], arr.at[core, z], x_sem.at[1]).start()
        pltpu.make_async_copy(prof.at[i], junk.at[0], x_sem.at[0]).start()

    def gather():
        for d, c in order:
            lev = 2 * lax.rem(z + d, nz) + (core + c) % 2
            i = pair_on(b // 2, lev, ng, -1)
            run(4, functools.partial(pick, i))
            if (d, c) == (0, 0):
                run(5, functools.partial(comm_profile_own, i))
            else:
                run(5, functools.partial(comm_profile, i, lev))

    run(4, gather)

    share = pltpu.make_async_remote_copy(
        src_ref=tabs.at[core],
        dst_ref=tabs.at[core],
        send_sem=tab_sem.at[2],
        recv_sem=tab_sem.at[3],
        device_id=(b, g + 1 - 2 * core),
        device_id_type=MESH,
    )

    def comm_share():
        pltpu.make_async_copy(tabs.at[0], tabs.at[0], tab_sem.at[1]).wait()
        share.start()

    run(5, comm_share)

    def turn_rinv():
        for i in range(channels // 128):
            line = rinv_v[:, i * 128 : (i + 1) * 128]
            rcol[i * 128 : (i + 1) * 128] = jnp.broadcast_to(line, (128, 128)).T

    run(6, turn_rinv)

    def comm_tabs_arrive():
        pltpu.make_async_copy(tabs.at[0], tabs.at[0], tab_sem.at[3]).wait()

    run(5, comm_tabs_arrive)

    def table(t):
        return tabs[:, :, t].reshape(ng * WIDTH, channels)

    def turn_tables():
        for t in range(NTAB):
            tabs_t[t] = table(t).T

    run(6, turn_tables)

    def comm_arr():
        pltpu.make_async_copy(arr, arr, x_sem.at[1]).wait()

    run(5, comm_arr)

    def observe():
        profiles = arr[...].reshape(ng * WIDTH, PAIR)
        kinds = jnp.concatenate(
            [inn_r[j, channels:].astype(F32)[0:1] for j in range(2)], axis=1
        )
        seen = jnp.concatenate([inn_r[j, 0:channels].astype(F32) for j in range(2)], axis=1)
        evolved = jnp.zeros((channels, PAIR), F32)
        for t in range(NTAB):
            evolved = jnp.where(kinds == t, dot(tabs_t[t], profiles, ((1,), (0,))), evolved)
        scale = jnp.concatenate([rcol[...]] * 2, axis=1)
        resid = scale * (evolved - seen)
        total = jnp.zeros((ng * WIDTH, PAIR), F32)
        for t in range(NTAB):
            masked = jnp.where(kinds == t, resid, 0.0).astype(BF16)
            total = total + dot(table(t), masked, ((1,), (0,)))
        back[...] = total.astype(BF16).reshape(2, nz, WIDTH, PAIR)

    run(5, comm_swap_arrive)
    run(7, observe)

    def comm_back():
        for d, c in order:
            oz, oc = lax.rem(z + d, nz), (core + c) % 2
            src = back.at[oc, oz]
            if (d, c) == (0, 0):
                pltpu.make_async_copy(src, home.at[from_pair], x_sem.at[3]).start()
                pltpu.make_async_copy(src, junk.at[1], x_sem.at[2]).start()
            else:
                pltpu.make_async_remote_copy(
                    src_ref=src,
                    dst_ref=home.at[from_pair],
                    send_sem=x_sem.at[2],
                    recv_sem=x_sem.at[3],
                    device_id=(b, 2 * oz + oc),
                    device_id_type=MESH,
                ).start()
        pltpu.make_async_copy(home, home, x_sem.at[3]).wait()

    run(8, comm_back)

    def spread_home(i):
        low = lon_low(col_row(i))
        block = home[i].astype(F32)
        at = pl.ds(pl.multiple_of(i * PAIR, PAIR), PAIR)
        for k in range(16):
            a_mat[k * WIDTH : (k + 1) * WIDTH, at] = jnp.where(low == k, block, 0.0).astype(BF16)

    def spread():
        pl.loop(0, nb // 2)(spread_home)

    run(9, spread)

    def scatter():
        sums = dot(a_mat[...], hot[...], ((1,), (1,)))
        for k in range(2):
            adj[k * 256 : (k + 1) * 256] = sums[:, k * LAT : (k + 1) * LAT]

    run(9, scatter)

    def weigh():
        for l in range(0, LEV, 2):
            firsts, lasts = [], []
            for k in (l, l + 1):
                tiles = []
                for f in range(FIELDS):
                    for i in range(LON // 8):
                        cells = adj[pl.ds(i * 8 * WIDTH + f * LEV + k, 8, stride=WIDTH)]
                        w = sig_v[f, k, 8 * i : 8 * i + 8].astype(F32) * cells
                        ua[f, HALO + k, 8 * i : 8 * i + 8] = w
                        tiles.append(w)
                firsts.append(jnp.where(upper, tiles[0], pltpu.roll(tiles[LON // 8], 4, 0)))
                lasts.append(jnp.where(upper, pltpu.roll(tiles[LON // 8 - 1], 4, 0), tiles[-1]))
            pack_w[0, l // 2] = jnp.concatenate(firsts, axis=0).astype(BF16)
            pack_w[1, l // 2] = jnp.concatenate(lasts, axis=0).astype(BF16)
            for k in (l, l + 1):
                if k < HALO or k >= LEV - HALO:
                    for f in range(FIELDS):
                        w_e[f, HALO + k] = ua[f, HALO + k, 0:LON].astype(BF16)

    run(9, weigh)

    halo2 = halo_copies(pack_w, lon_w, ((w_e, HALO, w_e),), w_send, w_recv)

    def comm_halo2():
        halo_start(*halo2)
        halo_arrive(*halo2)

    run(10, comm_halo2)

    def widen_w():
        for i in range(LEV // 2 + 2):
            for k in (0, 1):
                e = 1 + 2 * i + k
                first = lon_w[0, i].astype(F32)[8 * k : 8 * k + 8]
                last = lon_w[1, i].astype(F32)[8 * k : 8 * k + 8]
                ua[0, e, LON:] = jnp.where(upper, first, pltpu.roll(last, 4, 0))
                ua[1, e, LON:] = jnp.where(upper, pltpu.roll(first, 4, 0), last)
        for f in range(FIELDS):
            for e in range(EXT):
                if e < HALO or e >= HALO + LEV:
                    ua[f, e, 0:LON] = w_e[f, e].astype(F32)

    run(11, widen_w)

    def scale_level(e):
        for f in range(FIELDS):
            ub[f, e] = dfx[f, e] * ua[f, e]

    def backward(src, dst, step):
        for e in range(step, EXT - step):
            for f in range(FIELDS):
                w = ua[f, e] + lap(src, f, e)
                ua[f, e] = w
                dst[f, e] = dfx[f, e] * w

    def finish(l):
        for f in range(FIELDS):
            e = l + HALO
            w = (ua[f, e] + lap(ub, f, e))[0:LON]
            out_v[f, l] = inc_e[f, e].astype(F32) + w

    def diffuse_back():
        for e in range(EXT):
            scale_level(e)
        backward(ub, uc, 1)
        backward(uc, ub, 2)
        for l in range(LEV):
            finish(l)

    run(11, diffuse_back)
    result = pltpu.make_async_copy(out_v, out_hbm, load_sem.at[8])
    result.start()

    def comm_tabs_gone():
        if nz > 1:
            gone = tabs.at[0, 0 : nz - 1]
            pltpu.make_async_copy(gone, gone, tab_sem.at[0]).wait()
        share.wait_send()

    def comm_profiles_gone():
        pltpu.make_async_copy(prof, prof, x_sem.at[0]).wait()

    def comm_home_gone():
        pltpu.make_async_copy(back, back, x_sem.at[2]).wait()

    def comm_halo_gone():
        halo_sent(*halo)

    def comm_halo2_gone():
        halo_sent(*halo2)

    run(1, comm_halo_gone)
    run(5, comm_swap_gone)
    run(5, comm_tabs_gone)
    run(5, comm_profiles_gone)
    run(8, comm_home_gone)
    run(10, comm_halo2_gone)
    result.wait()


def body(
    nb,
    ng,
    increment,
    diffusivity,
    sigma,
    jacobian,
    rinv,
    innovation,
    obs_column,
    obs_table,
    obs_count,
):
    channels = jacobian.shape[1]
    tables = jnp.transpose(jacobian, (0, 2, 3, 1)).reshape(NTAB, WIDTH, channels)
    nz = ng // 2
    hbm = pl.BlockSpec(memory_space=pltpu.HBM)
    dma = pltpu.SemaphoreType.DMA
    extended = pltpu.VMEM((FIELDS, EXT, LON, LAT), BF16)
    wide = pltpu.VMEM((FIELDS, EXT, ROWS, LAT), F32)
    return pl.pallas_call(
        functools.partial(kernel, nb, ng),
        out_shape=jax.ShapeDtypeStruct((FIELDS, LEV, LON, LAT), F32),
        in_specs=[hbm] * 9,
        out_specs=hbm,
        scratch_shapes=[
            pltpu.VMEM((FIELDS, LEV, LON, LAT), F32),
            extended,
            extended,
            pltpu.VMEM((FIELDS, LEV, LON, LAT), BF16),
            pltpu.VMEM((1, channels), F32),
            pltpu.SMEM((1, nb), jnp.int32),
            pltpu.VMEM((nb, CAP), jnp.int32),
            pltpu.VMEM((nb, CAP), jnp.int32),
            pltpu.VMEM((channels, min(16, nb), CAP), BF16),
            pltpu.VMEM((channels * min(16, nb), CAP), F32),
            pltpu.VMEM((2, channels + 16, CAP), BF16),
            pltpu.VMEM((2, channels + 16, CAP), BF16),
            pltpu.VMEM((2, LEV, 16, LAT), BF16),
            pltpu.VMEM((2, EXT, 16, LAT), BF16),
            pltpu.VMEM((2, LEV // 2, 16, LAT), BF16),
            pltpu.VMEM((2, LEV // 2 + 2, 16, LAT), BF16),
            extended,
            wide,
            wide,
            wide,
            wide,
            pltpu.VMEM((WIDTH * LON, LAT), F32),
            pltpu.VMEM((16 * WIDTH, 2 * LAT), BF16),
            pltpu.VMEM((2 * LAT, nb * CAP), BF16),
            pltpu.VMEM((16 * WIDTH, nb * CAP), BF16),
            pltpu.VMEM((WIDTH * LON, LAT), F32),
            pltpu.VMEM((ng, WIDTH, PAIR), BF16),
            pltpu.VMEM((2, nz, WIDTH, PAIR), BF16),
            pltpu.VMEM((2, WIDTH, PAIR), BF16),
            pltpu.VMEM((2, nz, NTAB, WIDTH, channels), BF16),
            pltpu.VMEM((NTAB, channels, ng * WIDTH), BF16),
            pltpu.VMEM((channels, CAP), F32),
            pltpu.VMEM((2, nz, WIDTH, PAIR), BF16),
            pltpu.VMEM((ng, WIDTH, PAIR), BF16),
            dma((9,)),
            dma((10,)),
            dma((10,)),
            dma((10,)),
            dma((10,)),
            dma((4,)),
            dma((4,)),
            dma((3,)),
        ],
        compiler_params=pltpu.CompilerParams(
            collective_id=0, has_side_effects=True, vmem_limit_bytes=60 * 1024 * 1024
        ),
    )(
        increment,
        diffusivity,
        sigma,
        tables,
        rinv.reshape(1, channels),
        innovation,
        obs_column,
        obs_table,
        obs_count,
    )


def solution(mesh):
    in_specs = (
        P(None, "lev", "band", None),
        P(None, "lev", "band", None),
        P(None, "lev", "band", None),
        P(None, None, None, "lev"),
        P(),
        P("band", None, None, None),
        P("band", None, None),
        P("band", None, None),
        P("band", None),
    )
    out_specs = P(None, "lev", "band", None)
    run = functools.partial(body, mesh.shape["band"], mesh.shape["lev"])
    return jax.shard_map(run, mesh=mesh, in_specs=in_specs, out_specs=out_specs, check_vma=False)
```

```python
import functools

import jax
import jax.numpy as jnp
from jax import lax
from jax.experimental import pallas as pl
from jax.experimental.pallas import tpu as pltpu
from jax.sharding import PartitionSpec as P

MESH = pl.DeviceIdType.MESH
F32 = jnp.float32
BF16 = jnp.bfloat16

NTAB = 4
STEPS = 3
HALO = 3
FIELDS = 2
LEV = 8
LON = 32
LAT = 128
CAP = 128
ROWS = LON + 8
EXT = LEV + 2 * HALO
WIDTH = FIELDS * LEV
PAIR = 2 * CAP


def dot(a, b, dims):
    return lax.dot_general(a, b, (dims, ((), ())), preferred_element_type=F32)


def gap(lev, ng):
    rank = ng - 1 - lev
    if ng != 16:
        return 0, rank, 1, ng
    long, short = rank // 4, rank % 4
    turn = lambda k: k + (k >= 2).astype(jnp.int32) - 2 * (k >= 3).astype(jnp.int32)
    return turn(short), turn(long), 4, 4


def pair_on(pair, lev, ng, sign):
    dx, dy, nx, ny = gap(lev, ng)
    x = lax.rem(pair // ny + nx + sign * dx, nx)
    y = lax.rem(pair % ny + ny + sign * dy, ny)
    return x * ny + y


def run(step, work):
    work()


def kernel(
    nb,
    ng,
    inc_hbm,
    dif_hbm,
    sig_hbm,
    jac_hbm,
    rinv_hbm,
    inn_hbm,
    col_hbm,
    tab_hbm,
    cnt_hbm,
    out_v,
    inc_e,
    dif_e,
    sig_v,
    rinv_v,
    cnt_s,
    col_v,
    cols,
    tab_v,
    inn_v,
    inn_f,
    inn_s,
    inn_r,
    pack,
    lon_r,
    pack_w,
    lon_w,
    w_e,
    dfx,
    ua,
    ub,
    uc,
    st,
    s_mat,
    hot,
    hot_t,
    a_mat,
    adj,
    prof,
    arr,
    junk,
    tabs,
    tabs_t,
    rcol,
    back,
    home,
    load_sem,
    halo_send,
    halo_recv,
    w_send,
    w_recv,
    tab_sem,
    x_sem,
    swap_sem,
):
    b, g = lax.axis_index("band"), lax.axis_index("lev")
    nz = ng // 2
    z, core = g // 2, g % 2
    left, right = lax.rem(b + nb - 1, nb), lax.rem(b + 1, nb)
    to_pair = pair_on(b // 2, g, ng, 1)
    from_pair = pair_on(b // 2, g, ng, -1)
    own_pair = to_pair == b // 2
    has_low, has_high = g > 0, g < ng - 1
    channels = inn_v.shape[0]
    inn_rows = inn_v.shape[1]

    hops = sorted(range(nz), key=lambda d: -min(d, nz - d))
    order = [(d, c) for d in hops for c in (0, 1) if (d, c) != (0, 0)] + [(0, 0)]

    place = {at: k for k, at in enumerate(order)}
    groups = {}
    for k, (d, c) in enumerate(order):
        groups.setdefault(max(1, min(d, nz - d)), []).append(k)
    groups = [(dist, min(ks), max(ks) + 1) for dist, ks in sorted(groups.items())]
    levs = [2 * lax.rem(z + d, nz) + (core + c) % 2 for d, c in order]
    owners = [pair_on(b // 2, lev, ng, -1) for lev in levs]

    loads = [
        pltpu.make_async_copy(inc_hbm, inc_e.at[:, HALO : HALO + LEV], load_sem.at[0]),
        pltpu.make_async_copy(dif_hbm, dif_e.at[:, HALO : HALO + LEV], load_sem.at[1]),
        pltpu.make_async_copy(col_hbm.at[0], col_v, load_sem.at[2]),
        pltpu.make_async_copy(sig_hbm, sig_v, load_sem.at[3]),
        pltpu.make_async_copy(tab_hbm.at[0], tab_v, load_sem.at[4]),
        pltpu.make_async_copy(rinv_hbm, rinv_v, load_sem.at[5]),
        pltpu.make_async_copy(cnt_hbm, cnt_s, load_sem.at[6]),
        pltpu.make_async_copy(
            inn_hbm.at[
                0,
                :,
                pl.ds(pl.multiple_of((2 * to_pair) // inn_rows * inn_rows, inn_rows), inn_rows),
            ],
            inn_v,
            load_sem.at[7],
        ),
    ]
    l_inc, l_dif, l_col, l_sig, l_tab, l_rinv, l_cnt, l_inn = loads

    barrier = pltpu.get_barrier_semaphore()

    def greet(band, lev):
        pl.semaphore_signal(barrier, inc=1, device_id=(band, lev), device_id_type=MESH)

    def comm_greet():
        for d, c in order[:-1]:
            greet(b, 2 * lax.rem(z + d, nz) + (core + c) % 2)
        for j in range(2):

            @pl.when(2 * from_pair + j != b)
            def _():
                greet(2 * from_pair + j, g)

        for has, lev in ((has_low, g - 1), (has_high, g + 1)):

            @pl.when(has)
            def _():
                for side in (left, right):
                    greet(side, lev)

        for side in (left, right):
            greet(side, g)

    def start_loads():
        for load in loads:
            load.start()

    run(0, comm_greet)
    run(0, start_loads)

    zeros = jnp.zeros((FIELDS, HALO, LON, LAT), BF16)
    zeros_lon = jnp.zeros((2, HALO, 16, LAT), BF16)

    def clear():
        for edge, at in ((0, slice(0, HALO)), (ng - 1, slice(EXT - HALO, EXT))):

            @pl.when(g == edge)
            def _():
                inc_e[:, at] = zeros
                dif_e[:, at] = zeros
                w_e[:, at] = zeros
                lon_r[:, at] = zeros_lon
                lon_w[:, 0 if edge == 0 else LEV // 2 + 1] = zeros_lon[:, 0]

        for e in (0, EXT - 1):
            lon_r[:, e] = zeros_lon[:, 0]
            for f in range(FIELDS):
                ua[f, e, LON:] = jnp.zeros((8, LAT), F32)

    run(0, clear)

    sub = lax.broadcasted_iota(jnp.int32, (8, LAT), 0)
    upper = sub < 4

    def pack_level(l):
        for side in (0, 1):
            tiles = []
            for f in range(FIELDS):
                x = inc_e[f, HALO + l].astype(F32)
                d = dif_e[f, HALO + l].astype(F32)
                if side == 0:
                    tile = jnp.where(upper, x[0:8], pltpu.roll(d[0:8], 4, 0))
                else:
                    tile = jnp.where(upper, pltpu.roll(d[LON - 8 :], 4, 0), x[LON - 8 :])
                tiles.append(tile)
            pack[side, l] = jnp.concatenate(tiles, axis=0).astype(BF16)

    def packing():
        for l in range(LEV):
            pack_level(l)

    def wait_fields():
        l_inc.wait()
        l_dif.wait()

    run(0, wait_fields)
    run(0, packing)

    def comm_barrier():
        senders = (
            2
            + 2 * has_low.astype(jnp.int32)
            + 2 * has_high.astype(jnp.int32)
            + (ng - 1)
            + 2
            - own_pair.astype(jnp.int32)
        )
        pl.semaphore_wait(barrier, senders)

    run(0, comm_barrier)

    def halo_copies(strips, lon_to, lev_pairs, send, recv):
        def copy(k, src, dst, band, lev):
            return pltpu.make_async_remote_copy(
                src_ref=src,
                dst_ref=dst,
                send_sem=send.at[k],
                recv_sem=recv.at[k],
                device_id=(band, lev),
                device_id_type=MESH,
            )

        level, up, down = [], [], []
        sides = (left, right)
        count = strips.shape[1]
        edge = 2 * count // LEV
        base = (lon_to.shape[1] - count) // 2
        for k in (0, 1):
            level.append(copy(k, strips.at[k], lon_to.at[k, base : base + count], sides[k], g))
            up.append(
                copy(2 + k, strips.at[k, count - edge :], lon_to.at[k, base - edge : base], sides[k], g + 1)
            )
            down.append(
                copy(
                    4 + k,
                    strips.at[k, 0:edge],
                    lon_to.at[k, base + count : base + count + edge],
                    sides[k],
                    g - 1,
                )
            )
        for i, (src, first, dst) in enumerate(lev_pairs):
            up.append(
                copy(6 + i, src.at[:, first + LEV - HALO : first + LEV], dst.at[:, 0:HALO], b, g + 1)
            )
            down.append(
                copy(8 + i, src.at[:, first : first + HALO], dst.at[:, EXT - HALO :], b, g - 1)
            )
        return level, up, down

    def halo_start(level, up, down):
        for part in (slice(0, 2), slice(2, None)):
            for has, copies in ((has_high, up), (has_low, down)):

                @pl.when(has)
                def _():
                    for c in copies[part]:
                        c.start()

            if part.start == 0:
                for c in level:
                    c.start()

    def halo_arrive(level, up, down):
        for c in level:
            c.wait_recv()
        for has, copies in ((has_low, up), (has_high, down)):

            @pl.when(has)
            def _():
                for c in copies:
                    c.wait_recv()

    def halo_sent(level, up, down):
        for c in level:
            c.wait_send()
        for has, copies in ((has_high, up), (has_low, down)):

            @pl.when(has)
            def _():
                for c in copies:
                    c.wait_send()

    halo = halo_copies(
        pack, lon_r, ((inc_hbm, 0, inc_e), (dif_hbm, 0, dif_e)), halo_send, halo_recv
    )

    def comm_halo():
        halo_start(*halo)

    run(1, comm_halo)

    def comm_tabs():
        pltpu.make_async_copy(jac_hbm, tabs.at[core, z], tab_sem.at[1]).start()

        for d in hops[:-1]:
            pltpu.make_async_remote_copy(
                src_ref=jac_hbm,
                dst_ref=tabs.at[core, z],
                send_sem=tab_sem.at[0],
                recv_sem=tab_sem.at[1],
                device_id=(b, 2 * lax.rem(z + d, nz) + core),
                device_id_type=MESH,
            ).start()

    run(5, comm_tabs)

    def wait_observations():
        l_inn.wait()
        l_tab.wait()
        l_rinv.wait()
        l_cnt.wait()

    run(0, wait_observations)

    def spread_inn(i):
        at = pl.ds(pl.multiple_of(i * 8, 8), 8)
        inn_f[pl.ds(pl.multiple_of(i * 8 * inn_rows, 8 * inn_rows), 8 * inn_rows)] = (
            inn_v[at].astype(F32).reshape(8 * inn_rows, CAP)
        )

    def innovations():
        pl.loop(0, channels // 8)(spread_inn)
        row = lax.rem(2 * to_pair, inn_rows)
        slot_id = lax.broadcasted_iota(jnp.int32, (16, CAP), 1)
        for j in range(2):
            for i in range(channels // 16):
                halves = [
                    inn_f[pl.ds((2 * i + k) * 8 * inn_rows + row + j, 8, stride=inn_rows)]
                    for k in range(2)
                ]
                inn_s[j, 16 * i : 16 * i + 16] = jnp.concatenate(halves, axis=0).astype(BF16)
            kinds = jnp.broadcast_to(tab_v[pl.ds(2 * to_pair + j, 1)], (16, CAP))
            kinds = jnp.where(slot_id < cnt_s[0, 2 * to_pair + j], kinds, -1)
            inn_s[j, channels:] = kinds.astype(F32).astype(BF16)

    run(6, innovations)

    def swap_copy(j):
        return pltpu.make_async_remote_copy(
            src_ref=inn_s.at[j],
            dst_ref=inn_r.at[b % 2],
            send_sem=swap_sem.at[j],
            recv_sem=swap_sem.at[2],
            device_id=(2 * to_pair + j, g),
            device_id_type=MESH,
        )

    def comm_swap():
        for j in range(2):
            here = 2 * to_pair + j == b

            @pl.when(here)
            def _():
                pltpu.make_async_copy(inn_s.at[j], inn_r.at[b % 2], swap_sem.at[2]).start()

            @pl.when(jnp.logical_not(here))
            def _():
                swap_copy(j).start()

    def comm_swap_gone():
        for j in range(2):

            @pl.when(2 * to_pair + j != b)
            def _():
                swap_copy(j).wait_send()

    def comm_swap_arrive():
        pltpu.make_async_copy(inn_r, inn_r, swap_sem.at[2]).wait()

    run(5, comm_swap)

    def sort_cols():
        for k, i in enumerate(owners):
            cols[k : k + 1] = jnp.concatenate(
                [col_v[pl.ds(2 * i, 1)], col_v[pl.ds(2 * i + 1, 1)]], axis=1
            )

    def lon_low(line):
        return lax.shift_right_logical(line, 7) & 15

    def build_hot(k):
        line = cols[pl.ds(k, 1)]
        want = (lax.shift_right_logical(line, 11) & 1) * LAT + (line & (LAT - 1))
        iota = lax.broadcasted_iota(jnp.int32, (2 * LAT, PAIR), 0)
        hot[:, pl.ds(pl.multiple_of(k * PAIR, PAIR), PAIR)] = jnp.where(
            iota == want, 1.0, 0.0
        ).astype(BF16)

    def make_hot():
        pl.loop(0, ng)(build_hot)

    run(0, l_col.wait)
    run(0, sort_cols)
    run(2, make_hot)

    def comm_halo_arrive():
        halo_arrive(*halo)

    run(1, comm_halo_arrive)

    def widen_level(e):
        first = lon_r[0, e].astype(F32)
        last = lon_r[1, e].astype(F32)
        for f in range(FIELDS):
            r = first[8 * f : 8 * f + 8]
            l = last[8 * f : 8 * f + 8]
            ua[f, e, LON:] = jnp.where(upper, r, l)
            dfx[f, e, LON:] = pltpu.roll(jnp.where(upper, l, r), 4, 0)
            ua[f, e, 0:LON] = inc_e[f, e].astype(F32)
            dfx[f, e, 0:LON] = dif_e[f, e].astype(F32)

    def widen():
        for e in range(EXT):
            widen_level(e)

    run(3, widen)

    lane = lax.broadcasted_iota(jnp.int32, (ROWS, LAT), 1)

    def lap(ref, f, e):
        c = ref[f, e]
        total = ref[f, e - 1] + ref[f, e + 1]
        total = total + (pltpu.roll(c, 1, 0) + pltpu.roll(c, ROWS - 1, 0))
        total = total + jnp.where(lane == 0, 0.0, pltpu.roll(c, 1, 1))
        total = total + jnp.where(lane == LAT - 1, 0.0, pltpu.roll(c, LAT - 1, 1))
        return total - 6.0 * c

    def forward(src, dst, step):
        for e in range(step, EXT - step):
            for f in range(FIELDS):
                dst[f, e] = src[f, e] + dfx[f, e] * lap(src, f, e)

    def last_step(l):
        for f in range(FIELDS):
            e = l + HALO
            field = (uc[f, e] + dfx[f, e] * lap(uc, f, e))[0:LON]
            st[(f * LEV + l) * LON : (f * LEV + l + 1) * LON] = (
                sig_v[f, l].astype(F32) * field
            )

    def diffuse():
        forward(ua, ub, 1)
        forward(ub, uc, 2)
        for l in range(LEV):
            last_step(l)

    run(0, l_sig.wait)
    run(3, diffuse)

    def lay_out():
        for lon in range(LON):
            parts = [st[pl.ds(f * LEV * LON + lon, LEV, stride=LON)] for f in range(FIELDS)]
            s_mat[
                (lon % 16) * WIDTH : (lon % 16 + 1) * WIDTH,
                (lon // 16) * LAT : (lon // 16 + 1) * LAT,
            ] = jnp.concatenate(parts, axis=0).astype(BF16)

    run(4, lay_out)

    def pick(k):
        low = lon_low(cols[k : k + 1])
        rows = dot(s_mat[...], hot[:, k * PAIR : (k + 1) * PAIR], ((1,), (0,)))
        total = jnp.zeros((WIDTH, PAIR), F32)
        for n in range(16):
            total = jnp.where(low == n, rows[n * WIDTH : (n + 1) * WIDTH], total)
        prof[k] = total.astype(BF16)

    def comm_profile(k):
        if order[k] == (0, 0):
            pltpu.make_async_copy(prof.at[k], arr.at[core, z], x_sem.at[1]).start()
            pltpu.make_async_copy(prof.at[k], junk.at[0], x_sem.at[0]).start()
        else:
            pltpu.make_async_remote_copy(
                src_ref=prof.at[k],
                dst_ref=arr.at[core, z],
                send_sem=x_sem.at[0],
                recv_sem=x_sem.at[1],
                device_id=(b, levs[k]),
                device_id_type=MESH,
            ).start()

    def gather():
        for k in range(ng):
            run(4, functools.partial(pick, k))
            run(5, functools.partial(comm_profile, k))

    run(4, gather)

    share = pltpu.make_async_remote_copy(
        src_ref=tabs.at[core],
        dst_ref=tabs.at[core],
        send_sem=tab_sem.at[2],
        recv_sem=tab_sem.at[3],
        device_id=(b, g + 1 - 2 * core),
        device_id_type=MESH,
    )

    def comm_share():
        pltpu.make_async_copy(tabs.at[0], tabs.at[0], tab_sem.at[1]).wait()
        share.start()

    run(5, comm_share)

    def turn_rinv():
        for i in range(channels // 128):
            line = rinv_v[:, i * 128 : (i + 1) * 128]
            rcol[i * 128 : (i + 1) * 128] = jnp.broadcast_to(line, (128, 128)).T

    run(6, turn_rinv)

    def comm_tabs_arrive():
        pltpu.make_async_copy(tabs.at[0], tabs.at[0], tab_sem.at[3]).wait()

    run(5, comm_tabs_arrive)

    def table(t):
        return tabs[:, :, t].reshape(ng * WIDTH, channels)

    def turn_tables():
        for t in range(NTAB):
            tabs_t[t] = table(t).T

    run(6, turn_tables)

    def turn_hot():
        for k in range(ng):
            at = slice(k * PAIR, (k + 1) * PAIR)
            hot_t[at] = hot[:, at].T

    run(6, turn_hot)

    def comm_arr():
        pltpu.make_async_copy(arr, arr, x_sem.at[1]).wait()

    run(5, comm_arr)

    def observe():
        profiles = arr[...].reshape(ng * WIDTH, PAIR)
        kinds = jnp.concatenate(
            [inn_r[j, channels:].astype(F32)[0:1] for j in range(2)], axis=1
        )
        seen = jnp.concatenate([inn_r[j, 0:channels].astype(F32) for j in range(2)], axis=1)
        evolved = jnp.zeros((channels, PAIR), F32)
        for t in range(NTAB):
            evolved = jnp.where(kinds == t, dot(tabs_t[t], profiles, ((1,), (0,))), evolved)
        scale = jnp.concatenate([rcol[...]] * 2, axis=1)
        resid = scale * (evolved - seen)
        total = jnp.zeros((ng * WIDTH, PAIR), F32)
        for t in range(NTAB):
            masked = jnp.where(kinds == t, resid, 0.0).astype(BF16)
            total = total + dot(table(t), masked, ((1,), (0,)))
        back[...] = total.astype(BF16).reshape(2, nz, WIDTH, PAIR)

    run(5, comm_swap_arrive)
    run(7, observe)

    def comm_back():
        for k, (d, c) in enumerate(order):
            src = back.at[(core + c) % 2, lax.rem(z + d, nz)]
            there = place[(nz - d) % nz, c]
            arrives = x_sem.at[2 + max(1, min(d, nz - d))]
            if (d, c) == (0, 0):
                pltpu.make_async_copy(src, home.at[there], arrives).start()
                pltpu.make_async_copy(src, junk.at[1], x_sem.at[2]).start()
            else:
                pltpu.make_async_remote_copy(
                    src_ref=src,
                    dst_ref=home.at[there],
                    send_sem=x_sem.at[2],
                    recv_sem=arrives,
                    device_id=(b, levs[k]),
                    device_id_type=MESH,
                ).start()

    run(8, comm_back)

    def comm_home(dist, lo, hi):
        part = home.at[lo:hi]
        pltpu.make_async_copy(part, part, x_sem.at[2 + dist]).wait()

    def spread(lo, hi):
        for k in range(lo, hi):
            low = jnp.broadcast_to(lon_low(cols[k : k + 1]).astype(F32), (WIDTH, PAIR)).astype(BF16)
            block = home[k]
            for n in range(16):
                a_mat[n * WIDTH : (n + 1) * WIDTH, k * PAIR : (k + 1) * PAIR] = jnp.where(
                    low == jnp.asarray(n, BF16), block, jnp.zeros_like(block)
                )

    def scatter(lo, hi):
        at = slice(lo * PAIR, hi * PAIR)
        part = dot(a_mat[:, at], hot_t[at], ((1,), (0,)))
        for k in range(2):
            half = part[:, k * LAT : (k + 1) * LAT]
            rows = slice(k * 16 * WIDTH, (k + 1) * 16 * WIDTH)
            if lo == groups[0][1]:
                adj[rows] = half
            else:
                adj[rows] += half

    for group in groups:
        run(8, functools.partial(comm_home, *group))
        run(9, functools.partial(spread, *group[1:]))
        run(9, functools.partial(scatter, *group[1:]))

    def weigh():
        for l in range(0, LEV, 2):
            firsts, lasts = [], []
            for k in (l, l + 1):
                tiles = []
                for f in range(FIELDS):
                    for i in range(LON // 8):
                        cells = adj[pl.ds(i * 8 * WIDTH + f * LEV + k, 8, stride=WIDTH)]
                        w = sig_v[f, k, 8 * i : 8 * i + 8].astype(F32) * cells
                        ua[f, HALO + k, 8 * i : 8 * i + 8] = w
                        tiles.append(w)
                firsts.append(jnp.where(upper, tiles[0], pltpu.roll(tiles[LON // 8], 4, 0)))
                lasts.append(jnp.where(upper, pltpu.roll(tiles[LON // 8 - 1], 4, 0), tiles[-1]))
            pack_w[0, l // 2] = jnp.concatenate(firsts, axis=0).astype(BF16)
            pack_w[1, l // 2] = jnp.concatenate(lasts, axis=0).astype(BF16)
            for k in (l, l + 1):
                if k < HALO or k >= LEV - HALO:
                    for f in range(FIELDS):
                        w_e[f, HALO + k] = ua[f, HALO + k, 0:LON].astype(BF16)

    run(9, weigh)

    halo2 = halo_copies(pack_w, lon_w, ((w_e, HALO, w_e),), w_send, w_recv)

    def comm_halo2():
        halo_start(*halo2)
        halo_arrive(*halo2)

    run(10, comm_halo2)

    def widen_w():
        for i in range(LEV // 2 + 2):
            for k in (0, 1):
                e = 1 + 2 * i + k
                first = lon_w[0, i].astype(F32)[8 * k : 8 * k + 8]
                last = lon_w[1, i].astype(F32)[8 * k : 8 * k + 8]
                ua[0, e, LON:] = jnp.where(upper, first, pltpu.roll(last, 4, 0))
                ua[1, e, LON:] = jnp.where(upper, pltpu.roll(first, 4, 0), last)
        for f in range(FIELDS):
            for e in range(EXT):
                if e < HALO or e >= HALO + LEV:
                    ua[f, e, 0:LON] = w_e[f, e].astype(F32)

    run(11, widen_w)

    def scale_level(e):
        for f in range(FIELDS):
            ub[f, e] = dfx[f, e] * ua[f, e]

    def backward(src, dst, step):
        for e in range(step, EXT - step):
            for f in range(FIELDS):
                w = ua[f, e] + lap(src, f, e)
                ua[f, e] = w
                dst[f, e] = dfx[f, e] * w

    def finish(l):
        for f in range(FIELDS):
            e = l + HALO
            w = (ua[f, e] + lap(ub, f, e))[0:LON]
            out_v[f, l] = inc_e[f, e].astype(F32) + w

    def diffuse_back():
        for e in range(EXT):
            scale_level(e)
        backward(ub, uc, 1)
        backward(uc, ub, 2)
        for l in range(LEV):
            finish(l)

    run(11, diffuse_back)

    def comm_tabs_gone():
        if nz > 1:
            gone = tabs.at[0, 0 : nz - 1]
            pltpu.make_async_copy(gone, gone, tab_sem.at[0]).wait()
        share.wait_send()

    def comm_profiles_gone():
        pltpu.make_async_copy(prof, prof, x_sem.at[0]).wait()

    def comm_home_gone():
        pltpu.make_async_copy(back, back, x_sem.at[2]).wait()

    def comm_halo_gone():
        halo_sent(*halo)

    def comm_halo2_gone():
        halo_sent(*halo2)

    run(1, comm_halo_gone)
    run(5, comm_swap_gone)
    run(5, comm_tabs_gone)
    run(5, comm_profiles_gone)
    run(8, comm_home_gone)
    run(10, comm_halo2_gone)


def body(
    nb,
    ng,
    increment,
    diffusivity,
    sigma,
    jacobian,
    rinv,
    innovation,
    obs_column,
    obs_table,
    obs_count,
):
    channels = jacobian.shape[1]
    tables = jnp.transpose(jacobian, (0, 2, 3, 1)).reshape(NTAB, WIDTH, channels)
    nz = ng // 2
    hbm = pl.BlockSpec(memory_space=pltpu.HBM)
    dma = pltpu.SemaphoreType.DMA
    extended = pltpu.VMEM((FIELDS, EXT, LON, LAT), BF16)
    wide = pltpu.VMEM((FIELDS, EXT, ROWS, LAT), F32)
    return pl.pallas_call(
        functools.partial(kernel, nb, ng),
        out_shape=pltpu.VMEM((FIELDS, LEV, LON, LAT), F32),
        in_specs=[hbm] * 9,
        out_specs=pl.BlockSpec(memory_space=pltpu.VMEM),
        scratch_shapes=[
            extended,
            extended,
            pltpu.VMEM((FIELDS, LEV, LON, LAT), BF16),
            pltpu.VMEM((1, channels), F32),
            pltpu.SMEM((1, nb), jnp.int32),
            pltpu.VMEM((nb, CAP), jnp.int32),
            pltpu.VMEM((ng, PAIR), jnp.int32),
            pltpu.VMEM((nb, CAP), jnp.int32),
            pltpu.VMEM((channels, min(16, nb), CAP), BF16),
            pltpu.VMEM((channels * min(16, nb), CAP), F32),
            pltpu.VMEM((2, channels + 16, CAP), BF16),
            pltpu.VMEM((2, channels + 16, CAP), BF16),
            pltpu.VMEM((2, LEV, 16, LAT), BF16),
            pltpu.VMEM((2, EXT, 16, LAT), BF16),
            pltpu.VMEM((2, LEV // 2, 16, LAT), BF16),
            pltpu.VMEM((2, LEV // 2 + 2, 16, LAT), BF16),
            extended,
            wide,
            wide,
            wide,
            wide,
            pltpu.VMEM((WIDTH * LON, LAT), F32),
            pltpu.VMEM((16 * WIDTH, 2 * LAT), BF16),
            pltpu.VMEM((2 * LAT, nb * CAP), BF16),
            pltpu.VMEM((nb * CAP, 2 * LAT), BF16),
            pltpu.VMEM((16 * WIDTH, nb * CAP), BF16),
            pltpu.VMEM((WIDTH * LON, LAT), F32),
            pltpu.VMEM((ng, WIDTH, PAIR), BF16),
            pltpu.VMEM((2, nz, WIDTH, PAIR), BF16),
            pltpu.VMEM((2, WIDTH, PAIR), BF16),
            pltpu.VMEM((2, nz, NTAB, WIDTH, channels), BF16),
            pltpu.VMEM((NTAB, channels, ng * WIDTH), BF16),
            pltpu.VMEM((channels, CAP), F32),
            pltpu.VMEM((2, nz, WIDTH, PAIR), BF16),
            pltpu.VMEM((ng, WIDTH, PAIR), BF16),
            dma((8,)),
            dma((10,)),
            dma((10,)),
            dma((10,)),
            dma((10,)),
            dma((4,)),
            dma((7,)),
            dma((3,)),
        ],
        compiler_params=pltpu.CompilerParams(
            collective_id=0, has_side_effects=True, vmem_limit_bytes=60 * 1024 * 1024
        ),
    )(
        increment,
        diffusivity,
        sigma,
        tables,
        rinv.reshape(1, channels),
        innovation,
        obs_column,
        obs_table,
        obs_count,
    )


def solution(mesh):
    in_specs = (
        P(None, "lev", "band", None),
        P(None, "lev", "band", None),
        P(None, "lev", "band", None),
        P(None, None, None, "lev"),
        P(),
        P("band", None, None, None),
        P("band", None, None),
        P("band", None, None),
        P("band", None),
    )
    out_specs = P(None, "lev", "band", None)
    run = functools.partial(body, mesh.shape["band"], mesh.shape["lev"])
    return jax.shard_map(run, mesh=mesh, in_specs=in_specs, out_specs=out_specs, check_vma=False)
```

```python
import functools

import jax
import jax.numpy as jnp
from jax import lax
from jax.experimental import pallas as pl
from jax.experimental.pallas import tpu as pltpu
from jax.sharding import PartitionSpec as P

MESH = pl.DeviceIdType.MESH
F32 = jnp.float32
BF16 = jnp.bfloat16

NTAB = 4
STEPS = 3
HALO = 3
FIELDS = 2
LEV = 8
LON = 32
LAT = 128
CAP = 128
ROWS = LON + 8
EXT = LEV + 2 * HALO
WIDTH = FIELDS * LEV
PAIR = 2 * CAP


def dot(a, b, dims):
    return lax.dot_general(a, b, (dims, ((), ())), preferred_element_type=F32)


def gap(lev, ng):
    rank = ng - 1 - lev
    if ng != 16:
        return 0, rank, 1, ng
    long, short = rank // 4, rank % 4
    turn = lambda k: k + (k >= 2).astype(jnp.int32) - 2 * (k >= 3).astype(jnp.int32)
    return turn(short), turn(long), 4, 4


def pair_on(pair, lev, ng, sign):
    dx, dy, nx, ny = gap(lev, ng)
    x = lax.rem(pair // ny + nx + sign * dx, nx)
    y = lax.rem(pair % ny + ny + sign * dy, ny)
    return x * ny + y


def run(step, work):
    work()


def kernel(
    nb,
    ng,
    inc_hbm,
    dif_hbm,
    sig_hbm,
    jac_hbm,
    rinv_hbm,
    inn_hbm,
    col_hbm,
    tab_hbm,
    cnt_hbm,
    out_v,
    inc_e,
    dif_e,
    sig_v,
    rinv_v,
    cnt_s,
    col_v,
    cols,
    tab_v,
    inn_v,
    inn_f,
    inn_s,
    inn_r,
    pack,
    lon_r,
    pack_w,
    lon_w,
    w_e,
    dfx,
    ua,
    ub,
    uc,
    st,
    s_mat,
    hot,
    hot_t,
    a_mat,
    adj,
    prof,
    arr,
    junk,
    tabs,
    tabs_t,
    rcol,
    back,
    home,
    load_sem,
    halo_send,
    halo_recv,
    w_send,
    w_recv,
    tab_sem,
    x_sem,
    swap_sem,
):
    b, g = lax.axis_index("band"), lax.axis_index("lev")
    nz = ng // 2
    z, core = g // 2, g % 2
    left, right = lax.rem(b + nb - 1, nb), lax.rem(b + 1, nb)
    to_pair = pair_on(b // 2, g, ng, 1)
    from_pair = pair_on(b // 2, g, ng, -1)
    own_pair = to_pair == b // 2
    has_low, has_high = g > 0, g < ng - 1
    channels = inn_v.shape[0]
    inn_rows = inn_v.shape[1]

    hops = sorted(range(nz), key=lambda d: -min(d, nz - d))
    order = [(d, c) for d in hops for c in (0, 1) if (d, c) != (0, 0)] + [(0, 0)]

    place = {at: k for k, at in enumerate(order)}
    groups = {}
    for k, (d, c) in enumerate(order):
        groups.setdefault(max(1, min(d, nz - d)), []).append(k)
    groups = [(dist, min(ks), max(ks) + 1) for dist, ks in sorted(groups.items())]
    levs = [2 * lax.rem(z + d, nz) + (core + c) % 2 for d, c in order]
    owners = [pair_on(b // 2, lev, ng, -1) for lev in levs]

    loads = [
        pltpu.make_async_copy(inc_hbm, inc_e.at[:, HALO : HALO + LEV], load_sem.at[0]),
        pltpu.make_async_copy(dif_hbm, dif_e.at[:, HALO : HALO + LEV], load_sem.at[1]),
        pltpu.make_async_copy(col_hbm.at[0], col_v, load_sem.at[2]),
        pltpu.make_async_copy(sig_hbm, sig_v, load_sem.at[3]),
        pltpu.make_async_copy(tab_hbm.at[0], tab_v, load_sem.at[4]),
        pltpu.make_async_copy(rinv_hbm, rinv_v, load_sem.at[5]),
        pltpu.make_async_copy(cnt_hbm, cnt_s, load_sem.at[6]),
        pltpu.make_async_copy(
            inn_hbm.at[
                0,
                :,
                pl.ds(pl.multiple_of((2 * to_pair) // inn_rows * inn_rows, inn_rows), inn_rows),
            ],
            inn_v,
            load_sem.at[7],
        ),
    ]
    l_inc, l_dif, l_col, l_sig, l_tab, l_rinv, l_cnt, l_inn = loads

    barrier = pltpu.get_barrier_semaphore()

    def greet(band, lev):
        pl.semaphore_signal(barrier, inc=1, device_id=(band, lev), device_id_type=MESH)

    def comm_greet():
        for d, c in order[:-1]:
            greet(b, 2 * lax.rem(z + d, nz) + (core + c) % 2)
        for j in range(2):

            @pl.when(2 * from_pair + j != b)
            def _():
                greet(2 * from_pair + j, g)

        for has, lev in ((has_low, g - 1), (has_high, g + 1)):

            @pl.when(has)
            def _():
                for side in (left, right):
                    greet(side, lev)

        for side in (left, right):
            greet(side, g)

    def start_first():
        l_inc.start()
        l_dif.start()

    def start_loads():
        for load in loads[2:]:
            load.start()

    run(0, start_first)
    run(0, comm_greet)
    run(0, start_loads)

    zeros = jnp.zeros((FIELDS, HALO, LON, LAT), BF16)
    zeros_lon = jnp.zeros((2, HALO, 16, LAT), BF16)

    def clear():
        for edge, at in ((0, slice(0, HALO)), (ng - 1, slice(EXT - HALO, EXT))):

            @pl.when(g == edge)
            def _():
                inc_e[:, at] = zeros
                dif_e[:, at] = zeros
                w_e[:, at] = zeros
                lon_r[:, at] = zeros_lon
                lon_w[:, 0 if edge == 0 else LEV // 2 + 1] = zeros_lon[:, 0]

        for e in (0, EXT - 1):
            lon_r[:, e] = zeros_lon[:, 0]
            for f in range(FIELDS):
                ua[f, e, LON:] = jnp.zeros((8, LAT), F32)

    run(0, clear)

    sub = lax.broadcasted_iota(jnp.int32, (8, LAT), 0)
    upper = sub < 4

    def pack_level(l):
        for side in (0, 1):
            tiles = []
            for f in range(FIELDS):
                x = inc_e[f, HALO + l].astype(F32)
                d = dif_e[f, HALO + l].astype(F32)
                if side == 0:
                    tile = jnp.where(upper, x[0:8], pltpu.roll(d[0:8], 4, 0))
                else:
                    tile = jnp.where(upper, pltpu.roll(d[LON - 8 :], 4, 0), x[LON - 8 :])
                tiles.append(tile)
            pack[side, l] = jnp.concatenate(tiles, axis=0).astype(BF16)

    def packing():
        for l in range(LEV):
            pack_level(l)

    def wait_fields():
        l_inc.wait()
        l_dif.wait()

    run(0, wait_fields)
    run(0, packing)

    def comm_barrier():
        senders = (
            2
            + 2 * has_low.astype(jnp.int32)
            + 2 * has_high.astype(jnp.int32)
            + (ng - 1)
            + 2
            - own_pair.astype(jnp.int32)
        )
        pl.semaphore_wait(barrier, senders)

    run(0, comm_barrier)

    def halo_copies(strips, lon_to, lev_pairs, send, recv):
        def copy(k, src, dst, band, lev):
            return pltpu.make_async_remote_copy(
                src_ref=src,
                dst_ref=dst,
                send_sem=send.at[k],
                recv_sem=recv.at[k],
                device_id=(band, lev),
                device_id_type=MESH,
            )

        level, up, down = [], [], []
        sides = (left, right)
        count = strips.shape[1]
        edge = 2 * count // LEV
        base = (lon_to.shape[1] - count) // 2
        for k in (0, 1):
            level.append(copy(k, strips.at[k], lon_to.at[k, base : base + count], sides[k], g))
            up.append(
                copy(2 + k, strips.at[k, count - edge :], lon_to.at[k, base - edge : base], sides[k], g + 1)
            )
            down.append(
                copy(
                    4 + k,
                    strips.at[k, 0:edge],
                    lon_to.at[k, base + count : base + count + edge],
                    sides[k],
                    g - 1,
                )
            )
        for i, (src, first, dst) in enumerate(lev_pairs):
            up.append(
                copy(6 + i, src.at[:, first + LEV - HALO : first + LEV], dst.at[:, 0:HALO], b, g + 1)
            )
            down.append(
                copy(8 + i, src.at[:, first : first + HALO], dst.at[:, EXT - HALO :], b, g - 1)
            )
        return level, up, down

    def halo_start(level, up, down):
        for part in (slice(0, 2), slice(2, None)):
            for has, copies in ((has_high, up), (has_low, down)):

                @pl.when(has)
                def _():
                    for c in copies[part]:
                        c.start()

            if part.start == 0:
                for c in level:
                    c.start()

    def halo_arrive(level, up, down):
        for c in level:
            c.wait_recv()
        for has, copies in ((has_low, up), (has_high, down)):

            @pl.when(has)
            def _():
                for c in copies:
                    c.wait_recv()

    def halo_sent(level, up, down):
        for c in level:
            c.wait_send()
        for has, copies in ((has_high, up), (has_low, down)):

            @pl.when(has)
            def _():
                for c in copies:
                    c.wait_send()

    halo = halo_copies(
        pack, lon_r, ((inc_e, HALO, inc_e), (dif_e, HALO, dif_e)), halo_send, halo_recv
    )

    def comm_halo():
        halo_start(*halo)

    run(1, comm_halo)

    def comm_tabs():
        pltpu.make_async_copy(jac_hbm, tabs.at[core, z], tab_sem.at[1]).start()

        for d in hops[:-1]:
            pltpu.make_async_remote_copy(
                src_ref=jac_hbm,
                dst_ref=tabs.at[core, z],
                send_sem=tab_sem.at[0],
                recv_sem=tab_sem.at[1],
                device_id=(b, 2 * lax.rem(z + d, nz) + core),
                device_id_type=MESH,
            ).start()


    def wait_observations():
        l_inn.wait()
        l_tab.wait()
        l_rinv.wait()
        l_cnt.wait()

    run(0, wait_observations)

    def spread_inn(i):
        at = pl.ds(pl.multiple_of(i * 8, 8), 8)
        inn_f[pl.ds(pl.multiple_of(i * 8 * inn_rows, 8 * inn_rows), 8 * inn_rows)] = (
            inn_v[at].astype(F32).reshape(8 * inn_rows, CAP)
        )

    def innovations():
        pl.loop(0, channels // 8)(spread_inn)
        row = lax.rem(2 * to_pair, inn_rows)
        slot_id = lax.broadcasted_iota(jnp.int32, (16, CAP), 1)
        for j in range(2):
            for i in range(channels // 16):
                halves = [
                    inn_f[pl.ds((2 * i + k) * 8 * inn_rows + row + j, 8, stride=inn_rows)]
                    for k in range(2)
                ]
                inn_s[j, 16 * i : 16 * i + 16] = jnp.concatenate(halves, axis=0).astype(BF16)
            kinds = jnp.broadcast_to(tab_v[pl.ds(2 * to_pair + j, 1)], (16, CAP))
            kinds = jnp.where(slot_id < cnt_s[0, 2 * to_pair + j], kinds, -1)
            inn_s[j, channels:] = kinds.astype(F32).astype(BF16)

    run(6, innovations)

    def swap_copy(j):
        return pltpu.make_async_remote_copy(
            src_ref=inn_s.at[j],
            dst_ref=inn_r.at[b % 2],
            send_sem=swap_sem.at[j],
            recv_sem=swap_sem.at[2],
            device_id=(2 * to_pair + j, g),
            device_id_type=MESH,
        )

    def comm_swap():
        for j in range(2):
            here = 2 * to_pair + j == b

            @pl.when(here)
            def _():
                pltpu.make_async_copy(inn_s.at[j], inn_r.at[b % 2], swap_sem.at[2]).start()

            @pl.when(jnp.logical_not(here))
            def _():
                swap_copy(j).start()

    def comm_swap_gone():
        for j in range(2):

            @pl.when(2 * to_pair + j != b)
            def _():
                swap_copy(j).wait_send()

    def comm_swap_arrive():
        pltpu.make_async_copy(inn_r, inn_r, swap_sem.at[2]).wait()

    run(5, comm_swap)

    def sort_cols():
        for k, i in enumerate(owners):
            cols[k : k + 1] = jnp.concatenate(
                [col_v[pl.ds(2 * i, 1)], col_v[pl.ds(2 * i + 1, 1)]], axis=1
            )

    def lon_low(line):
        return lax.shift_right_logical(line, 7) & 15

    def build_hot(k):
        line = cols[pl.ds(k, 1)]
        want = (lax.shift_right_logical(line, 11) & 1) * LAT + (line & (LAT - 1))
        iota = lax.broadcasted_iota(jnp.int32, (2 * LAT, PAIR), 0)
        hot[:, pl.ds(pl.multiple_of(k * PAIR, PAIR), PAIR)] = jnp.where(
            iota == want, 1.0, 0.0
        ).astype(BF16)

    def make_hot():
        pl.loop(0, ng)(build_hot)

    run(0, l_col.wait)
    run(0, sort_cols)
    run(2, make_hot)
    run(5, comm_tabs)

    def comm_halo_arrive():
        halo_arrive(*halo)

    run(1, comm_halo_arrive)

    def widen_level(e):
        first = lon_r[0, e].astype(F32)
        last = lon_r[1, e].astype(F32)
        for f in range(FIELDS):
            r = first[8 * f : 8 * f + 8]
            l = last[8 * f : 8 * f + 8]
            ua[f, e, LON:] = jnp.where(upper, r, l)
            dfx[f, e, LON:] = pltpu.roll(jnp.where(upper, l, r), 4, 0)
            ua[f, e, 0:LON] = inc_e[f, e].astype(F32)
            dfx[f, e, 0:LON] = dif_e[f, e].astype(F32)

    def widen():
        for e in range(EXT):
            widen_level(e)

    run(3, widen)

    lane = lax.broadcasted_iota(jnp.int32, (ROWS, LAT), 1)

    def lap(ref, f, e):
        c = ref[f, e]
        total = ref[f, e - 1] + ref[f, e + 1]
        total = total + (pltpu.roll(c, 1, 0) + pltpu.roll(c, ROWS - 1, 0))
        total = total + jnp.where(lane == 0, 0.0, pltpu.roll(c, 1, 1))
        total = total + jnp.where(lane == LAT - 1, 0.0, pltpu.roll(c, LAT - 1, 1))
        return total - 6.0 * c

    def forward(src, dst, step):
        for e in range(step, EXT - step):
            for f in range(FIELDS):
                dst[f, e] = src[f, e] + dfx[f, e] * lap(src, f, e)

    def last_step(l):
        for f in range(FIELDS):
            e = l + HALO
            field = (uc[f, e] + dfx[f, e] * lap(uc, f, e))[0:LON]
            st[(f * LEV + l) * LON : (f * LEV + l + 1) * LON] = (
                sig_v[f, l].astype(F32) * field
            )

    def diffuse():
        forward(ua, ub, 1)
        forward(ub, uc, 2)
        for l in range(LEV):
            last_step(l)

    run(0, l_sig.wait)
    run(3, diffuse)

    def lay_out():
        for lon in range(LON):
            parts = [st[pl.ds(f * LEV * LON + lon, LEV, stride=LON)] for f in range(FIELDS)]
            s_mat[
                (lon % 16) * WIDTH : (lon % 16 + 1) * WIDTH,
                (lon // 16) * LAT : (lon // 16 + 1) * LAT,
            ] = jnp.concatenate(parts, axis=0).astype(BF16)

    run(4, lay_out)

    def pick(k):
        low = lon_low(cols[k : k + 1])
        rows = dot(s_mat[...], hot[:, k * PAIR : (k + 1) * PAIR], ((1,), (0,)))
        total = jnp.zeros((WIDTH, PAIR), F32)
        for n in range(16):
            total = jnp.where(low == n, rows[n * WIDTH : (n + 1) * WIDTH], total)
        prof[k] = total.astype(BF16)

    def comm_profile(k):
        if order[k] == (0, 0):
            pltpu.make_async_copy(prof.at[k], arr.at[core, z], x_sem.at[1]).start()
            pltpu.make_async_copy(prof.at[k], junk.at[0], x_sem.at[0]).start()
        else:
            pltpu.make_async_remote_copy(
                src_ref=prof.at[k],
                dst_ref=arr.at[core, z],
                send_sem=x_sem.at[0],
                recv_sem=x_sem.at[1],
                device_id=(b, levs[k]),
                device_id_type=MESH,
            ).start()

    def gather():
        for k in range(ng):
            run(4, functools.partial(pick, k))
            run(5, functools.partial(comm_profile, k))

    run(4, gather)

    share = pltpu.make_async_remote_copy(
        src_ref=tabs.at[core],
        dst_ref=tabs.at[core],
        send_sem=tab_sem.at[2],
        recv_sem=tab_sem.at[3],
        device_id=(b, g + 1 - 2 * core),
        device_id_type=MESH,
    )

    def comm_share():
        pltpu.make_async_copy(tabs.at[0], tabs.at[0], tab_sem.at[1]).wait()
        share.start()

    run(5, comm_share)

    def turn_rinv():
        for i in range(channels // 128):
            line = rinv_v[:, i * 128 : (i + 1) * 128]
            rcol[i * 128 : (i + 1) * 128] = jnp.broadcast_to(line, (128, 128)).T

    run(6, turn_rinv)

    def comm_tabs_arrive():
        pltpu.make_async_copy(tabs.at[0], tabs.at[0], tab_sem.at[3]).wait()

    run(5, comm_tabs_arrive)

    def table(t):
        return tabs[:, :, t].reshape(ng * WIDTH, channels)

    def turn_tables():
        for t in range(NTAB):
            tabs_t[t] = table(t).T

    run(6, turn_tables)

    def turn_hot():
        for k in range(ng):
            at = slice(k * PAIR, (k + 1) * PAIR)
            hot_t[at] = hot[:, at].T

    run(6, turn_hot)

    def comm_arr():
        pltpu.make_async_copy(arr, arr, x_sem.at[1]).wait()

    run(5, comm_arr)

    def observe():
        profiles = arr[...].reshape(ng * WIDTH, PAIR)
        kinds = jnp.concatenate(
            [inn_r[j, channels:].astype(F32)[0:1] for j in range(2)], axis=1
        )
        seen = jnp.concatenate([inn_r[j, 0:channels].astype(F32) for j in range(2)], axis=1)
        evolved = jnp.zeros((channels, PAIR), F32)
        for t in range(NTAB):
            evolved = jnp.where(kinds == t, dot(tabs_t[t], profiles, ((1,), (0,))), evolved)
        scale = jnp.concatenate([rcol[...]] * 2, axis=1)
        resid = scale * (evolved - seen)
        total = jnp.zeros((ng * WIDTH, PAIR), F32)
        for t in range(NTAB):
            masked = jnp.where(kinds == t, resid, 0.0).astype(BF16)
            total = total + dot(table(t), masked, ((1,), (0,)))
        back[...] = total.astype(BF16).reshape(2, nz, WIDTH, PAIR)

    run(5, comm_swap_arrive)
    run(7, observe)

    def comm_back():
        for k, (d, c) in enumerate(order):
            src = back.at[(core + c) % 2, lax.rem(z + d, nz)]
            there = place[(nz - d) % nz, c]
            arrives = x_sem.at[2 + max(1, min(d, nz - d))]
            if (d, c) == (0, 0):
                pltpu.make_async_copy(src, home.at[there], arrives).start()
                pltpu.make_async_copy(src, junk.at[1], x_sem.at[2]).start()
            else:
                pltpu.make_async_remote_copy(
                    src_ref=src,
                    dst_ref=home.at[there],
                    send_sem=x_sem.at[2],
                    recv_sem=arrives,
                    device_id=(b, levs[k]),
                    device_id_type=MESH,
                ).start()

    run(8, comm_back)

    def comm_home(dist, lo, hi):
        part = home.at[lo:hi]
        pltpu.make_async_copy(part, part, x_sem.at[2 + dist]).wait()

    def spread(lo, hi):
        for k in range(lo, hi):
            low = jnp.broadcast_to(lon_low(cols[k : k + 1]).astype(F32), (WIDTH, PAIR)).astype(BF16)
            block = home[k]
            for n in range(16):
                a_mat[n * WIDTH : (n + 1) * WIDTH, k * PAIR : (k + 1) * PAIR] = jnp.where(
                    low == jnp.asarray(n, BF16), block, jnp.zeros_like(block)
                )

    def scatter(lo, hi):
        at = slice(lo * PAIR, hi * PAIR)
        part = dot(a_mat[:, at], hot_t[at], ((1,), (0,)))
        for k in range(2):
            half = part[:, k * LAT : (k + 1) * LAT]
            rows = slice(k * 16 * WIDTH, (k + 1) * 16 * WIDTH)
            if lo == groups[0][1]:
                adj[rows] = half
            else:
                adj[rows] += half

    for group in groups:
        run(8, functools.partial(comm_home, *group))
        run(9, functools.partial(spread, *group[1:]))
        run(9, functools.partial(scatter, *group[1:]))

    def weigh():
        for l in range(0, LEV, 2):
            firsts, lasts = [], []
            for k in (l, l + 1):
                tiles = []
                for f in range(FIELDS):
                    for i in range(LON // 8):
                        cells = adj[pl.ds(i * 8 * WIDTH + f * LEV + k, 8, stride=WIDTH)]
                        w = sig_v[f, k, 8 * i : 8 * i + 8].astype(F32) * cells
                        ua[f, HALO + k, 8 * i : 8 * i + 8] = w
                        tiles.append(w)
                firsts.append(jnp.where(upper, tiles[0], pltpu.roll(tiles[LON // 8], 4, 0)))
                lasts.append(jnp.where(upper, pltpu.roll(tiles[LON // 8 - 1], 4, 0), tiles[-1]))
            pack_w[0, l // 2] = jnp.concatenate(firsts, axis=0).astype(BF16)
            pack_w[1, l // 2] = jnp.concatenate(lasts, axis=0).astype(BF16)
            for k in (l, l + 1):
                if k < HALO or k >= LEV - HALO:
                    for f in range(FIELDS):
                        w_e[f, HALO + k] = ua[f, HALO + k, 0:LON].astype(BF16)

    run(9, weigh)

    halo2 = halo_copies(pack_w, lon_w, ((w_e, HALO, w_e),), w_send, w_recv)

    def comm_halo2():
        halo_start(*halo2)
        halo_arrive(*halo2)

    run(10, comm_halo2)

    def widen_w():
        for i in range(LEV // 2 + 2):
            for k in (0, 1):
                e = 1 + 2 * i + k
                first = lon_w[0, i].astype(F32)[8 * k : 8 * k + 8]
                last = lon_w[1, i].astype(F32)[8 * k : 8 * k + 8]
                ua[0, e, LON:] = jnp.where(upper, first, pltpu.roll(last, 4, 0))
                ua[1, e, LON:] = jnp.where(upper, pltpu.roll(first, 4, 0), last)
        for f in range(FIELDS):
            for e in range(EXT):
                if e < HALO or e >= HALO + LEV:
                    ua[f, e, 0:LON] = w_e[f, e].astype(F32)

    run(11, widen_w)

    def scale_level(e):
        for f in range(FIELDS):
            ub[f, e] = dfx[f, e] * ua[f, e]

    def backward(src, dst, step):
        for e in range(step, EXT - step):
            for f in range(FIELDS):
                w = ua[f, e] + lap(src, f, e)
                ua[f, e] = w
                dst[f, e] = dfx[f, e] * w

    def finish(l):
        for f in range(FIELDS):
            e = l + HALO
            w = (ua[f, e] + lap(ub, f, e))[0:LON]
            out_v[f, l] = inc_e[f, e].astype(F32) + w

    def diffuse_back():
        for e in range(EXT):
            scale_level(e)
        backward(ub, uc, 1)
        backward(uc, ub, 2)
        for l in range(LEV):
            finish(l)

    run(11, diffuse_back)

    def comm_tabs_gone():
        if nz > 1:
            gone = tabs.at[0, 0 : nz - 1]
            pltpu.make_async_copy(gone, gone, tab_sem.at[0]).wait()
        share.wait_send()

    def comm_profiles_gone():
        pltpu.make_async_copy(prof, prof, x_sem.at[0]).wait()

    def comm_home_gone():
        pltpu.make_async_copy(back, back, x_sem.at[2]).wait()

    def comm_halo_gone():
        halo_sent(*halo)

    def comm_halo2_gone():
        halo_sent(*halo2)

    run(1, comm_halo_gone)
    run(5, comm_swap_gone)
    run(5, comm_tabs_gone)
    run(5, comm_profiles_gone)
    run(8, comm_home_gone)
    run(10, comm_halo2_gone)


def body(
    nb,
    ng,
    increment,
    diffusivity,
    sigma,
    jacobian,
    rinv,
    innovation,
    obs_column,
    obs_table,
    obs_count,
):
    channels = jacobian.shape[1]
    tables = jnp.transpose(jacobian, (0, 2, 3, 1)).reshape(NTAB, WIDTH, channels)
    nz = ng // 2
    hbm = pl.BlockSpec(memory_space=pltpu.HBM)
    dma = pltpu.SemaphoreType.DMA
    extended = pltpu.VMEM((FIELDS, EXT, LON, LAT), BF16)
    wide = pltpu.VMEM((FIELDS, EXT, ROWS, LAT), F32)
    return pl.pallas_call(
        functools.partial(kernel, nb, ng),
        out_shape=pltpu.VMEM((FIELDS, LEV, LON, LAT), F32),
        in_specs=[hbm] * 9,
        out_specs=pl.BlockSpec(memory_space=pltpu.VMEM),
        scratch_shapes=[
            extended,
            extended,
            pltpu.VMEM((FIELDS, LEV, LON, LAT), BF16),
            pltpu.VMEM((1, channels), F32),
            pltpu.SMEM((1, nb), jnp.int32),
            pltpu.VMEM((nb, CAP), jnp.int32),
            pltpu.VMEM((ng, PAIR), jnp.int32),
            pltpu.VMEM((nb, CAP), jnp.int32),
            pltpu.VMEM((channels, min(16, nb), CAP), BF16),
            pltpu.VMEM((channels * min(16, nb), CAP), F32),
            pltpu.VMEM((2, channels + 16, CAP), BF16),
            pltpu.VMEM((2, channels + 16, CAP), BF16),
            pltpu.VMEM((2, LEV, 16, LAT), BF16),
            pltpu.VMEM((2, EXT, 16, LAT), BF16),
            pltpu.VMEM((2, LEV // 2, 16, LAT), BF16),
            pltpu.VMEM((2, LEV // 2 + 2, 16, LAT), BF16),
            extended,
            wide,
            wide,
            wide,
            wide,
            pltpu.VMEM((WIDTH * LON, LAT), F32),
            pltpu.VMEM((16 * WIDTH, 2 * LAT), BF16),
            pltpu.VMEM((2 * LAT, nb * CAP), BF16),
            pltpu.VMEM((nb * CAP, 2 * LAT), BF16),
            pltpu.VMEM((16 * WIDTH, nb * CAP), BF16),
            pltpu.VMEM((WIDTH * LON, LAT), F32),
            pltpu.VMEM((ng, WIDTH, PAIR), BF16),
            pltpu.VMEM((2, nz, WIDTH, PAIR), BF16),
            pltpu.VMEM((2, WIDTH, PAIR), BF16),
            pltpu.VMEM((2, nz, NTAB, WIDTH, channels), BF16),
            pltpu.VMEM((NTAB, channels, ng * WIDTH), BF16),
            pltpu.VMEM((channels, CAP), F32),
            pltpu.VMEM((2, nz, WIDTH, PAIR), BF16),
            pltpu.VMEM((ng, WIDTH, PAIR), BF16),
            dma((8,)),
            dma((10,)),
            dma((10,)),
            dma((10,)),
            dma((10,)),
            dma((4,)),
            dma((7,)),
            dma((3,)),
        ],
        compiler_params=pltpu.CompilerParams(
            collective_id=0, has_side_effects=True, vmem_limit_bytes=60 * 1024 * 1024
        ),
    )(
        increment,
        diffusivity,
        sigma,
        tables,
        rinv.reshape(1, channels),
        innovation,
        obs_column,
        obs_table,
        obs_count,
    )


def solution(mesh):
    in_specs = (
        P(None, "lev", "band", None),
        P(None, "lev", "band", None),
        P(None, "lev", "band", None),
        P(None, None, None, "lev"),
        P(),
        P("band", None, None, None),
        P("band", None, None),
        P("band", None, None),
        P("band", None),
    )
    out_specs = P(None, "lev", "band", None)
    run = functools.partial(body, mesh.shape["band"], mesh.shape["lev"])
    return jax.shard_map(run, mesh=mesh, in_specs=in_specs, out_specs=out_specs, check_vma=False)
```
